32 devices in a mesh: dir: 2 (over core), seq: 16 (over z, y, x).
Axes of the slice: x: 2, y: 2, z: 4, core: 2. Of those that a mesh axis runs over, the one named last changes fastest.
Arguments:
- queries: bfloat16 [2, 4, 1024, 4096], P('dir', None, 'seq'), may hold values from -35 to 35
- key_states: bfloat16 [2, 4, 1024, 4096], P('dir', None, 'seq'), may hold values from -6 to 6
- value_vectors: bfloat16 [2, 4, 1024, 4096], P('dir', None, 'seq'), may hold values from -6 to 6
- hypothesis_lengths: int32 [4, 64], replicated, may hold values from 1 to 256, 1024 in all within a row
- join_weight: bfloat16 [8192, 2, 1024], P('seq', None, 'dir'), may hold values from -0.0625 to 0.0625
Outputs:
- joined: bfloat16 [4, 1024, 1024], P(None, 'seq', 'dir')
The draws below stay inside these ranges and needn't reach their ends.
All inputs are finite; a program needn't handle non-finite values.
Results may differ from the reference program's by a relative error of at most 0.0072.
Values may be sent and summed in bfloat16 or wider, within the bound.
A program may use at most 128 MiB of HBM per device.

```python
import math
import jax
import jax.numpy as jnp
import numpy as np
from jax import lax

MODEL_WIDTH = 4096
ATTENTION_HEADS = 32
PACKED_ROWS = 4
GROUP_HEADS = 8
JOIN_UNITS = 1024
LONGEST_TOKENS = 256
ROW_POSITIONS = 1024
ROW_HYPOTHESES = 64


def draw_queries(key, part):
    key = jax.random.fold_in(key, 11)
    array_shape = (2, PACKED_ROWS, ROW_POSITIONS, MODEL_WIDTH)
    values = jax.random.truncated_normal(key, -6.0, 6.0, array_shape, jnp.float32)
    return values.astype(jnp.bfloat16)


def draw_key_states(key, part):
    key = jax.random.fold_in(key, 23)
    array_shape = (2, PACKED_ROWS, ROW_POSITIONS, MODEL_WIDTH)
    values = jax.random.truncated_normal(key, -6.0, 6.0, array_shape, jnp.float32)
    return values.astype(jnp.bfloat16)


def block_levels(key, shape, pieces, low, largest):
    gain, own = 1.0, jax.random.fold_in(key, 6)
    for axis_at, shards_of in pieces:
        heights = jnp.exp(jax.random.uniform(jax.random.fold_in(own, axis_at), (shards_of,), jnp.float32, low / len(pieces), largest / len(pieces)))
        gain = gain * jnp.repeat(heights, shape[axis_at] // shards_of).reshape([-1 if axis == axis_at else 1 for axis in range(len(shape))])
    return gain


def profile(amount, total, limit, lean):
    weights = [(1 << 20) // math.isqrt(grade ** lean) + 1 for grade in range(2, amount + 1)]
    spare, holding = total - limit - (amount - 1), [1] * (amount - 1)
    while spare > 0:
        movable = [i for i in range(amount - 1) if holding[i] < limit]
        whole, left = sum([weights[i] for i in movable]), spare
        for i in movable:
            extra = min(limit - holding[i], max(1, left * weights[i] // whole), spare)
            holding[i] = holding[i] + extra
            spare = spare - extra
    return np.array([limit] + holding)


def ragged_sizes(rng, number_of, total, reach, lean):
    if number_of == 2:
        one = jax.random.randint(rng, (), max(1, total - reach), min(reach, total - 1) + 1)
        return jnp.stack([one, total - one])
    lengths = jnp.asarray(profile(number_of, total, reach, lean), jnp.int32)
    pairs = (number_of - 1) // 2
    donor, taker = lengths[1:1 + 2 * pairs:2], lengths[2:2 + 2 * pairs:2]
    room = jnp.minimum(donor - 1, reach - taker)
    shifted = jax.random.randint(jax.random.fold_in(rng, 1), (pairs,), 0, 1 << 20) % (room + 1)
    lengths = lengths.at[1:1 + 2 * pairs:2].set(donor - shifted).at[2:2 + 2 * pairs:2].set(taker + shifted)
    return lengths[jax.random.permutation(jax.random.fold_in(rng, 2), number_of)]


def normal_values(rng, dims, scale, most, pieces=(), held_as=jnp.bfloat16):
    entries = scale * jax.random.normal(rng, dims, jnp.float32)
    if pieces:
        entries = entries * block_levels(rng, dims, pieces, -0.22, 0.18)
    return jnp.clip(entries, -most, most).astype(held_as)


def setup_inputs(seed: int = 0) -> dict:
    key_of = jax.random.split(jax.random.key(seed), 6)
    queries = draw_queries(jax.random.fold_in(key_of[5], 71), 0)
    key_states = draw_key_states(jax.random.fold_in(key_of[5], 71), 0)
    value_vectors = normal_values(key_of[2], (2, PACKED_ROWS, ROW_POSITIONS, MODEL_WIDTH), 1.0, 6.0, ((0, 2), (2, 16)))
    hypothesis_lengths = jax.vmap(lambda own: ragged_sizes(own, ROW_HYPOTHESES, ROW_POSITIONS, LONGEST_TOKENS, 2))(jax.random.split(key_of[3], PACKED_ROWS)).reshape((PACKED_ROWS, ROW_HYPOTHESES)).astype(jnp.int32)
    join_weight = normal_values(key_of[4], (2 * MODEL_WIDTH, 2, JOIN_UNITS), (2 * MODEL_WIDTH) ** -0.5, 0.0625, ((0, 16), (2, 2)))
    return {"queries": queries, "key_states": key_states, "value_vectors": value_vectors, "hypothesis_lengths": hypothesis_lengths, "join_weight": join_weight}


def hypothesis_tables(length_list, row_len):
    length_list = length_list.astype(jnp.int32)
    ends = jnp.cumsum(length_list).astype(jnp.int32)
    starts = (ends - length_list).astype(jnp.int32)
    places = jnp.arange(row_len, dtype=jnp.int32)
    inside = (places[:, None] >= starts[None, :]) & (places[:, None] < ends[None, :])
    first = lax.optimization_barrier(jnp.sum(jnp.where(inside, starts[None, :], 0), axis=1)).astype(jnp.int32)
    after = lax.optimization_barrier(jnp.sum(jnp.where(inside, ends[None, :], 0), axis=1)).astype(jnp.int32)
    mirror = (first + after - 1 - places).astype(jnp.int32)
    return (first, mirror)

def attend_row(query_row, k_row, v_row, first):
    block_item = min(256, ROW_POSITIONS)
    token_span = min(block_item + LONGEST_TOKENS, ROW_POSITIONS)
    scale = 1.0 / math.sqrt(query_row.shape[2])

    def single_block(index):
        q_start = (index * block_item).astype(jnp.int32)
        k_start = jnp.maximum(q_start + block_item - token_span, 0).astype(jnp.int32)
        q_part = lax.dynamic_slice_in_dim(query_row, q_start, block_item, 0).astype(jnp.float32)
        k_part = lax.dynamic_slice_in_dim(k_row, k_start, token_span, 0).astype(jnp.float32)
        v_part = lax.dynamic_slice_in_dim(v_row, k_start, token_span, 0).astype(jnp.float32)
        scores = jnp.einsum('qhc,khc->hqk', q_part, k_part) * scale
        q_places = q_start + jnp.arange(block_item, dtype=jnp.int32)
        k_places = k_start + jnp.arange(token_span, dtype=jnp.int32)
        starts = lax.dynamic_slice_in_dim(first, q_start, block_item, 0)
        allowed = (k_places[None, :] >= starts[:, None]) & (k_places[None, :] <= q_places[:, None])
        scores = jnp.where(allowed[None], scores, jnp.float32(-1e+30))
        top = lax.optimization_barrier(jnp.max(scores, axis=2, keepdims=True))
        raised = jnp.exp(scores - top)
        weights = (raised / lax.optimization_barrier(jnp.sum(raised, axis=2, keepdims=True))).astype(jnp.bfloat16)
        weights = lax.optimization_barrier(weights).astype(jnp.float32)
        return jnp.einsum('hqk,khc->qhc', weights, v_part).astype(jnp.bfloat16)
    block_list = lax.map(single_block, jnp.arange(ROW_POSITIONS // block_item, dtype=jnp.int32))
    return block_list.reshape(ROW_POSITIONS, query_row.shape[1], query_row.shape[2])

def reference(queries, key_states, value_vectors, hypothesis_lengths, join_weight):
    head_width = MODEL_WIDTH // ATTENTION_HEADS
    leading_items, mirrored_items = jax.vmap(lambda length_list: hypothesis_tables(length_list, ROW_POSITIONS))(hypothesis_lengths)
    array_shape = (2 * PACKED_ROWS, ROW_POSITIONS, ATTENTION_HEADS, head_width)
    both_first = jnp.concatenate([leading_items, leading_items], axis=0)

    def per_row(items):
        return attend_row(items[0], items[1], items[2], items[3])
    context_vectors = lax.map(per_row, (queries.reshape(array_shape), key_states.reshape(array_shape), value_vectors.reshape(array_shape), both_first))
    context_vectors = context_vectors.reshape(2, PACKED_ROWS, ROW_POSITIONS, ATTENTION_HEADS, head_width)
    left_side = context_vectors[0]
    right_side = jnp.take_along_axis(context_vectors[1], mirrored_items[:, :, None, None], axis=1)
    feature_rows = jnp.stack([left_side, right_side], axis=3).reshape(PACKED_ROWS * ROW_POSITIONS, 2 * MODEL_WIDTH)
    matrix = join_weight.reshape(2 * MODEL_WIDTH, 2 * JOIN_UNITS)
    group_rows = 2 * GROUP_HEADS * head_width

    def append_group(grand_total, group):
        start = (group * group_rows).astype(jnp.int32)
        part_feat = lax.dynamic_slice_in_dim(feature_rows, start, group_rows, 1)
        part_weight = lax.dynamic_slice_in_dim(matrix, start, group_rows, 0)
        partial_value = jnp.dot(part_feat, part_weight, preferred_element_type=jnp.float32).astype(jnp.bfloat16)
        partial_value = lax.optimization_barrier(partial_value)
        return (grand_total + partial_value.astype(jnp.float32), None)
    grand_total, spare_tokens = lax.scan(append_group, jnp.zeros((PACKED_ROWS * ROW_POSITIONS, 2 * JOIN_UNITS), jnp.float32), jnp.arange(ATTENTION_HEADS // GROUP_HEADS, dtype=jnp.int32))
    joined = jax.nn.silu(grand_total[:, :JOIN_UNITS]) * grand_total[:, JOIN_UNITS:]
    return joined.astype(jnp.bfloat16).reshape(PACKED_ROWS, ROW_POSITIONS, JOIN_UNITS)
```

```python
import functools
import math

import jax
import jax.numpy as jnp
from jax import lax
from jax.experimental import pallas as pl
from jax.experimental.pallas import tpu as pltpu
from jax.sharding import PartitionSpec as P

ATTENTION_HEADS = 32
LONGEST_TOKENS = 256
PACKED_ROWS = 4


def swapped(array, axis, stride):
    return lax.ppermute(array, axis, [(i, i ^ 1 << stride) for i in range(lax.axis_size(axis))])


def hypothesis_tables(length_list, row_len):
    ends = jnp.cumsum(length_list)
    starts = ends - length_list
    places = jnp.arange(row_len, dtype=jnp.int32)
    inside = (places[:, None] >= starts[None, :]) & (places[:, None] < ends[None, :])
    first = jnp.sum(jnp.where(inside, starts[None, :], 0), axis=1)
    after = jnp.sum(jnp.where(inside, ends[None, :], 0), axis=1)
    mirror = first + after - 1 - places
    return (first, mirror)


def attend_group(query_row, k_row, v_row, first):
    row_len = query_row.shape[0]
    block_item = min(512, row_len)
    token_span = min(block_item + LONGEST_TOKENS, row_len)
    scale = 1.0 / math.sqrt(query_row.shape[2])

    def single_block(index):
        q_start = index * block_item
        k_start = jnp.maximum(q_start + block_item - token_span, 0)
        q_part = lax.dynamic_slice_in_dim(query_row, q_start, block_item, 0)
        k_part = lax.dynamic_slice_in_dim(k_row, k_start, token_span, 0)
        v_part = lax.dynamic_slice_in_dim(v_row, k_start, token_span, 0)
        scores = (
            jnp.einsum("qhc,khc->hqk", q_part, k_part, preferred_element_type=jnp.float32) * scale
        )
        q_places = q_start + jnp.arange(block_item, dtype=jnp.int32)
        k_places = k_start + jnp.arange(token_span, dtype=jnp.int32)
        starts = lax.dynamic_slice_in_dim(first, q_start, block_item, 0)
        allowed = (k_places[None, :] >= starts[:, None]) & (k_places[None, :] <= q_places[:, None])
        scores = jnp.where(allowed[None], scores, jnp.float32(-1e30))
        top = jnp.max(scores, axis=2, keepdims=True)
        raised = jnp.exp(scores - top)
        weights = (raised / jnp.sum(raised, axis=2, keepdims=True)).astype(jnp.bfloat16)
        return jnp.einsum(
            "hqk,khc->qhc", weights, v_part, preferred_element_type=jnp.float32
        ).astype(jnp.bfloat16)

    block_list = lax.map(single_block, jnp.arange(row_len // block_item, dtype=jnp.int32))
    return block_list.reshape(row_len, query_row.shape[1], query_row.shape[2])


def body(queries, key_states, value_vectors, hypothesis_lengths, join_weight):
    rows, piece, width = (queries.shape[1], queries.shape[2], queries.shape[3])
    devices = lax.axis_size("seq")
    groups = devices // rows
    head_width = width // ATTENTION_HEADS
    pair = width // groups
    heads_here = pair // head_width
    row_bits = rows.bit_length() - 1
    place = lax.axis_index("seq")
    row = place % rows
    row_len = devices * piece

    def regroup(states):
        states = states.reshape(rows, piece, groups, pair)
        return jnp.transpose(states, (2, 0, 1, 3)).reshape(groups * rows, piece, pair)

    q_all, k_all, v_all = (
        lax.all_to_all(regroup(queries[0]), "seq", split_axis=0, concat_axis=1, tiled=True),
        lax.all_to_all(regroup(key_states[0]), "seq", split_axis=0, concat_axis=1, tiled=True),
        lax.all_to_all(regroup(value_vectors[0]), "seq", split_axis=0, concat_axis=1, tiled=True),
    )
    block_rows = join_weight
    for bit in range(row_bits):
        partner = swapped(block_rows, "seq", bit)
        lower = place // 2**bit % 2 == 0
        block_rows = jnp.where(
            lower,
            jnp.concatenate([block_rows, partner], 0),
            jnp.concatenate([partner, block_rows], 0),
        )
    length_list = lax.dynamic_index_in_dim(hypothesis_lengths, row, 0, keepdims=False)
    first, mirror = hypothesis_tables(length_list, row_len)
    array_shape = (row_len, heads_here, head_width)
    context_vectors = attend_group(
        q_all.reshape(array_shape), k_all.reshape(array_shape), v_all.reshape(array_shape), first
    )
    other = swapped(context_vectors, "dir", 0)
    side = lax.axis_index("dir")
    left_side = jnp.where(side == 0, context_vectors, other)
    right_side = jnp.where(side == 0, other, context_vectors)
    right_side = jnp.take(right_side, mirror, axis=0)
    feature_rows = jnp.stack([left_side, right_side], axis=2).reshape(row_len, 2 * pair)
    columns = block_rows.shape[2]
    partial_value = jnp.dot(
        feature_rows, block_rows.reshape(2 * pair, 2 * columns), preferred_element_type=jnp.float32
    ).astype(jnp.bfloat16)
    arrived = lax.all_to_all(
        partial_value.reshape(devices, piece, 2 * columns),
        "seq",
        split_axis=0,
        concat_axis=0,
        tiled=True,
    )
    totals = jnp.sum(arrived.reshape(groups, rows, piece, 2 * columns).astype(jnp.float32), axis=0)
    joined = jax.nn.silu(totals[..., :columns]) * totals[..., columns:]
    return joined.astype(jnp.bfloat16)


def pair_kernel(
    geometry, first_ref, source_ref, q_ref, k_ref, v_ref, weight_ref, out_ref,
    states, weights, raw, feats, moves, bias, partials, arrived,
    send_sem, recv_sem, local_sem, wsend_sem, wrecv_sem, wlocal_sem,
    csend_sem, crecv_sem, psend_sem, precv_sem,
):
    devices, rows, groups, piece, head_width, chunks = geometry
    side = lax.axis_index("dir")
    me = lax.axis_index("seq")
    wide = 2 * head_width
    pair = chunks * wide
    row_len = devices * piece
    block = LONGEST_TOKENS
    blocks = row_len // block
    per_block = block // piece
    scale = 1.0 / math.sqrt(head_width)
    my_row = lax.rem(me, rows)
    my_group = lax.div(me, rows)

    def at(peer):
        return {"device_id": (side, peer), "device_id_type": pl.DeviceIdType.MESH}

    across = {"device_id": (1 - side, me), "device_id_type": pl.DeviceIdType.MESH}

    barrier = pltpu.get_barrier_semaphore()

    def greet(step, carry):
        pl.semaphore_signal(barrier, inc=1, **at(lax.rem(me + step, devices)))
        return carry

    lax.fori_loop(1, devices, greet, 0)
    pl.semaphore_signal(barrier, inc=1, **across)
    pl.semaphore_wait(barrier, devices)

    def own_piece(chunk, index, ref):
        return pltpu.make_async_copy(
            ref.at[0, my_row, :, pl.ds(pl.multiple_of(my_group * pair + chunk * wide, wide), wide)],
            states.at[chunk, index, pl.ds(pl.multiple_of(me * piece, piece), piece), :],
            local_sem.at[chunk],
        )

    def send_chunk(chunk, carry):
        def send_to(step, inner):
            peer = lax.rem(me + step, devices)
            row, group = lax.rem(peer, rows), lax.div(peer, rows)
            column = pl.multiple_of(group * pair + chunk * wide, wide)
            for index, ref in enumerate((q_ref, k_ref, v_ref)):
                pltpu.make_async_remote_copy(
                    src_ref=ref.at[0, row, :, pl.ds(column, wide)],
                    dst_ref=states.at[chunk, index, pl.ds(pl.multiple_of(me * piece, piece), piece), :],
                    send_sem=send_sem.at[chunk],
                    recv_sem=recv_sem.at[chunk],
                    **at(peer),
                ).start()
            return inner

        lax.fori_loop(1, devices, send_to, 0)
        for index, ref in enumerate((q_ref, k_ref, v_ref)):
            own_piece(chunk, index, ref).start()
        return carry

    lax.fori_loop(0, chunks, send_chunk, 0)

    def send_weights(step, carry):
        peer = my_group * rows + lax.rem(my_row + step, rows)
        pltpu.make_async_remote_copy(
            src_ref=weight_ref,
            dst_ref=weights.at[my_row],
            send_sem=wsend_sem,
            recv_sem=wrecv_sem,
            **at(peer),
        ).start()
        return carry

    lax.fori_loop(1, rows, send_weights, 0)
    own_weights = pltpu.make_async_copy(weight_ref, weights.at[my_row], wlocal_sem)
    own_weights.start()

    def tables(index, carry):
        start = pl.multiple_of(index * block, block)
        k_start = jnp.maximum(index - 1, 0) * block
        first = first_ref[pl.ds(start, block), :]
        source = source_ref[pl.ds(start, block), :]
        k_places = k_start + lax.broadcasted_iota(jnp.int32, (block, 2 * block), 1)
        q_places = start + lax.broadcasted_iota(jnp.int32, (block, 2 * block), 0)
        allowed = (k_places >= first) & (k_places <= q_places)
        bias[index] = jnp.where(allowed, jnp.float32(0), jnp.float32(-1e30))
        places = lax.broadcasted_iota(jnp.int32, (block, row_len), 1)
        moves[pl.ds(start, block), :] = jnp.where(places == source, 1.0, 0.0).astype(jnp.bfloat16)
        return carry

    lax.fori_loop(0, blocks, tables, 0)

    def exchange(chunk, head):
        column = pl.multiple_of((2 * head + side) * head_width, head_width)
        there = feats.at[chunk, :, pl.ds(column, head_width)]
        return pltpu.make_async_remote_copy(
            src_ref=there,
            dst_ref=there,
            send_sem=csend_sem.at[chunk, head],
            recv_sem=crecv_sem.at[chunk, head],
            **across,
        )

    def work_chunk(chunk, carry):
        others = states.at[chunk, :, pl.ds(0, row_len - piece), :]
        pltpu.make_async_copy(others, others, recv_sem.at[chunk]).wait()
        mine = states.at[chunk, :, pl.ds(0, piece), :]
        pltpu.make_async_copy(mine, mine, local_sem.at[chunk]).wait()

        def attend(index, inner):
            start = pl.multiple_of(index * block, block)
            k_start = pl.multiple_of(jnp.maximum(index - 1, 0) * block, block)
            for head in range(2):
                lanes = slice(head * head_width, (head + 1) * head_width)
                q_part = states[chunk, 0, pl.ds(start, block), lanes]
                k_part = states[chunk, 1, pl.ds(k_start, 2 * block), lanes]
                v_part = states[chunk, 2, pl.ds(k_start, 2 * block), lanes]
                scores = lax.dot_general(
                    q_part, k_part, (((1,), (1,)), ((), ())), preferred_element_type=jnp.float32
                )
                scores = scores * scale + bias[index]
                raised = jnp.exp(scores - jnp.max(scores, axis=1, keepdims=True))
                share = 1.0 / jnp.sum(raised, axis=1, keepdims=True)
                raw[pl.ds(start, block), lanes] = jnp.dot(
                    (raised * share).astype(jnp.bfloat16), v_part, preferred_element_type=jnp.float32
                ).astype(jnp.bfloat16)
            return inner

        lax.fori_loop(0, blocks, attend, 0)

        def mirror(index, inner):
            start = pl.multiple_of(index * block, block)
            moved = jnp.dot(
                moves[pl.ds(start, block), :], raw[...], preferred_element_type=jnp.float32
            ).astype(jnp.bfloat16)
            for head in range(2):
                column = pl.multiple_of((2 * head + side) * head_width, head_width)
                feats[chunk, pl.ds(start, block), pl.ds(column, head_width)] = moved[
                    :, head * head_width : (head + 1) * head_width
                ]
            return inner

        lax.fori_loop(0, blocks, mirror, 0)
        for head in range(2):
            exchange(chunk, head).start()
        return carry

    lax.fori_loop(0, chunks, work_chunk, 0)

    gathered = weights.at[pl.ds(0, rows - 1)]
    pltpu.make_async_copy(gathered, gathered, wrecv_sem).wait()
    own_weights.wait()

    def arrive(chunk, carry):
        for head in range(2):
            column = pl.multiple_of((2 * head + 1 - side) * head_width, head_width)
            there = feats.at[chunk, :, pl.ds(column, head_width)]
            pltpu.make_async_copy(there, there, crecv_sem.at[chunk, head]).wait()
        return carry

    lax.fori_loop(0, chunks, arrive, 0)

    def join(step, carry):
        index = lax.rem(lax.div(me, per_block) + 2 + step, blocks)
        start = pl.multiple_of(index * block, block)
        total = jnp.dot(
            feats[0, pl.ds(start, block), :], weights[0], preferred_element_type=jnp.float32
        )
        for chunk in range(1, chunks):
            total = total + jnp.dot(
                feats[chunk, pl.ds(start, block), :], weights[chunk], preferred_element_type=jnp.float32
            )
        rounded = total.astype(jnp.bfloat16)
        for part in range(per_block):
            peer = index * per_block + part
            partials[peer] = rounded[part * piece : (part + 1) * piece, :]

            @pl.when(peer != me)
            def _():
                pltpu.make_async_remote_copy(
                    src_ref=partials.at[peer],
                    dst_ref=arrived.at[me],
                    send_sem=psend_sem,
                    recv_sem=precv_sem,
                    **at(peer),
                ).start()

        return carry

    lax.fori_loop(0, blocks, join, 0)
    arrived[me] = partials[me]
    incoming = arrived.at[pl.ds(0, devices - 1)]
    pltpu.make_async_copy(incoming, incoming, precv_sem).wait()
    columns = out_ref.shape[2]
    for row in range(rows):
        total = arrived[row].astype(jnp.float32)
        for group in range(1, groups):
            total = total + arrived[group * rows + row].astype(jnp.float32)
        gate, up = total[:, :columns], total[:, columns:]
        out_ref[row] = (gate / (1.0 + jnp.exp(-gate)) * up).astype(jnp.bfloat16)

    def finish(chunk, carry):
        others = states.at[chunk, :, pl.ds(0, row_len - piece), :]
        pltpu.make_async_copy(others, others, send_sem.at[chunk]).wait()
        for head in range(2):
            exchange(chunk, head).wait_send()
        return carry

    lax.fori_loop(0, chunks, finish, 0)
    pltpu.make_async_copy(gathered, gathered, wsend_sem).wait()
    pltpu.make_async_copy(incoming, incoming, psend_sem).wait()


def fused_body(queries, key_states, value_vectors, hypothesis_lengths, join_weight):
    rows, piece, width = (queries.shape[1], queries.shape[2], queries.shape[3])
    devices = lax.axis_size("seq")
    groups = devices // rows
    head_width = width // ATTENTION_HEADS
    pair = width // groups
    wide = 2 * head_width
    chunks = pair // wide
    row_len = devices * piece
    blocks = row_len // LONGEST_TOKENS
    weight_rows, _, columns = join_weight.shape
    length_list = lax.dynamic_index_in_dim(
        hypothesis_lengths, lax.axis_index("seq") % rows, 0, keepdims=False
    )
    first, mirror = hypothesis_tables(length_list, row_len)
    places = jnp.arange(row_len, dtype=jnp.int32)
    source = jnp.where(lax.axis_index("dir") == 0, places, mirror)
    geometry = (devices, rows, groups, piece, head_width, chunks)
    return pl.pallas_call(
        functools.partial(pair_kernel, geometry),
        out_shape=jax.ShapeDtypeStruct((rows, piece, columns), jnp.bfloat16),
        in_specs=[pl.BlockSpec(memory_space=pltpu.VMEM)] * 2 + [pl.BlockSpec(memory_space=pl.ANY)] * 4,
        out_specs=pl.BlockSpec(memory_space=pltpu.VMEM),
        scratch_shapes=[
            pltpu.VMEM((chunks, 3, row_len, wide), jnp.bfloat16),
            pltpu.VMEM((chunks, weight_rows, 2 * columns), jnp.bfloat16),
            pltpu.VMEM((row_len, wide), jnp.bfloat16),
            pltpu.VMEM((chunks, row_len, 2 * wide), jnp.bfloat16),
            pltpu.VMEM((row_len, row_len), jnp.bfloat16),
            pltpu.VMEM((blocks, LONGEST_TOKENS, 2 * LONGEST_TOKENS), jnp.float32),
            pltpu.VMEM((devices, piece, 2 * columns), jnp.bfloat16),
            pltpu.VMEM((devices, piece, 2 * columns), jnp.bfloat16),
            pltpu.SemaphoreType.DMA((chunks,)),
            pltpu.SemaphoreType.DMA((chunks,)),
            pltpu.SemaphoreType.DMA((chunks,)),
            pltpu.SemaphoreType.DMA,
            pltpu.SemaphoreType.DMA,
            pltpu.SemaphoreType.DMA,
            pltpu.SemaphoreType.DMA((chunks, 2)),
            pltpu.SemaphoreType.DMA((chunks, 2)),
            pltpu.SemaphoreType.DMA,
            pltpu.SemaphoreType.DMA,
        ],
        compiler_params=pltpu.CompilerParams(
            collective_id=0, has_side_effects=True, vmem_limit_bytes=48 * 1024 * 1024
        ),
    )(
        first[:, None],
        source[:, None],
        queries,
        key_states,
        value_vectors,
        join_weight.reshape(weight_rows, 2 * columns),
    )


def fits_kernel(mesh):
    groups = mesh.shape["seq"] // PACKED_ROWS
    return ATTENTION_HEADS // groups == 2 * PACKED_ROWS


def solution(mesh):
    return jax.shard_map(
        fused_body if fits_kernel(mesh) else body,
        mesh=mesh,
        in_specs=(
            P("dir", None, "seq", None),
            P("dir", None, "seq", None),
            P("dir", None, "seq", None),
            P(),
            P("seq", None, "dir"),
        ),
        out_specs=P(None, "seq", "dir"),
        check_vma=False,
    )
```

```python
import functools
import math

import jax
import jax.numpy as jnp
from jax import lax
from jax.experimental import pallas as pl
from jax.experimental.pallas import tpu as pltpu
from jax.sharding import PartitionSpec as P

ATTENTION_HEADS = 32
LONGEST_TOKENS = 256
PACKED_ROWS = 4


def swapped(array, axis, stride):
    return lax.ppermute(array, axis, [(i, i ^ 1 << stride) for i in range(lax.axis_size(axis))])


def hypothesis_tables(length_list, row_len):
    ends = jnp.cumsum(length_list)
    starts = ends - length_list
    places = jnp.arange(row_len, dtype=jnp.int32)
    inside = (places[:, None] >= starts[None, :]) & (places[:, None] < ends[None, :])
    first = jnp.sum(jnp.where(inside, starts[None, :], 0), axis=1)
    after = jnp.sum(jnp.where(inside, ends[None, :], 0), axis=1)
    mirror = first + after - 1 - places
    return (first, mirror)


def attend_group(query_row, k_row, v_row, first):
    row_len = query_row.shape[0]
    block_item = min(512, row_len)
    token_span = min(block_item + LONGEST_TOKENS, row_len)
    scale = 1.0 / math.sqrt(query_row.shape[2])

    def single_block(index):
        q_start = index * block_item
        k_start = jnp.maximum(q_start + block_item - token_span, 0)
        q_part = lax.dynamic_slice_in_dim(query_row, q_start, block_item, 0)
        k_part = lax.dynamic_slice_in_dim(k_row, k_start, token_span, 0)
        v_part = lax.dynamic_slice_in_dim(v_row, k_start, token_span, 0)
        scores = (
            jnp.einsum("qhc,khc->hqk", q_part, k_part, preferred_element_type=jnp.float32) * scale
        )
        q_places = q_start + jnp.arange(block_item, dtype=jnp.int32)
        k_places = k_start + jnp.arange(token_span, dtype=jnp.int32)
        starts = lax.dynamic_slice_in_dim(first, q_start, block_item, 0)
        allowed = (k_places[None, :] >= starts[:, None]) & (k_places[None, :] <= q_places[:, None])
        scores = jnp.where(allowed[None], scores, jnp.float32(-1e30))
        top = jnp.max(scores, axis=2, keepdims=True)
        raised = jnp.exp(scores - top)
        weights = (raised / jnp.sum(raised, axis=2, keepdims=True)).astype(jnp.bfloat16)
        return jnp.einsum(
            "hqk,khc->qhc", weights, v_part, preferred_element_type=jnp.float32
        ).astype(jnp.bfloat16)

    block_list = lax.map(single_block, jnp.arange(row_len // block_item, dtype=jnp.int32))
    return block_list.reshape(row_len, query_row.shape[1], query_row.shape[2])


def body(queries, key_states, value_vectors, hypothesis_lengths, join_weight):
    rows, piece, width = (queries.shape[1], queries.shape[2], queries.shape[3])
    devices = lax.axis_size("seq")
    groups = devices // rows
    head_width = width // ATTENTION_HEADS
    pair = width // groups
    heads_here = pair // head_width
    row_bits = rows.bit_length() - 1
    place = lax.axis_index("seq")
    row = place % rows
    row_len = devices * piece

    def regroup(states):
        states = states.reshape(rows, piece, groups, pair)
        return jnp.transpose(states, (2, 0, 1, 3)).reshape(groups * rows, piece, pair)

    q_all, k_all, v_all = (
        lax.all_to_all(regroup(queries[0]), "seq", split_axis=0, concat_axis=1, tiled=True),
        lax.all_to_all(regroup(key_states[0]), "seq", split_axis=0, concat_axis=1, tiled=True),
        lax.all_to_all(regroup(value_vectors[0]), "seq", split_axis=0, concat_axis=1, tiled=True),
    )
    block_rows = join_weight
    for bit in range(row_bits):
        partner = swapped(block_rows, "seq", bit)
        lower = place // 2**bit % 2 == 0
        block_rows = jnp.where(
            lower,
            jnp.concatenate([block_rows, partner], 0),
            jnp.concatenate([partner, block_rows], 0),
        )
    length_list = lax.dynamic_index_in_dim(hypothesis_lengths, row, 0, keepdims=False)
    first, mirror = hypothesis_tables(length_list, row_len)
    array_shape = (row_len, heads_here, head_width)
    context_vectors = attend_group(
        q_all.reshape(array_shape), k_all.reshape(array_shape), v_all.reshape(array_shape), first
    )
    other = swapped(context_vectors, "dir", 0)
    side = lax.axis_index("dir")
    left_side = jnp.where(side == 0, context_vectors, other)
    right_side = jnp.where(side == 0, other, context_vectors)
    right_side = jnp.take(right_side, mirror, axis=0)
    feature_rows = jnp.stack([left_side, right_side], axis=2).reshape(row_len, 2 * pair)
    columns = block_rows.shape[2]
    partial_value = jnp.dot(
        feature_rows, block_rows.reshape(2 * pair, 2 * columns), preferred_element_type=jnp.float32
    ).astype(jnp.bfloat16)
    arrived = lax.all_to_all(
        partial_value.reshape(devices, piece, 2 * columns),
        "seq",
        split_axis=0,
        concat_axis=0,
        tiled=True,
    )
    totals = jnp.sum(arrived.reshape(groups, rows, piece, 2 * columns).astype(jnp.float32), axis=0)
    joined = jax.nn.silu(totals[..., :columns]) * totals[..., columns:]
    return joined.astype(jnp.bfloat16)


def pair_kernel(
    geometry, table_ref, q_ref, k_ref, v_ref, weight_ref, out_ref,
    states, queries_up, raw, own, up_from, up_into, down_from, down_into,
    own_stats, up_stats_from, up_stats_into, down_stats_from, down_stats_into,
    weights, feats, sums, partials, arrived, own_moves, up_moves, down_moves, own_bias, up_bias,
    send_sem, recv_sem, local_sem, qsend_sem, qrecv_sem, usend_sem, urecv_sem, dsend_sem, drecv_sem,
    wsend_sem, wrecv_sem, wlocal_sem, csend_sem, crecv_sem, psend_sem, precv_sem,
):
    planes, rows, members, piece, head_width, chunks = geometry
    side = lax.axis_index("dir")
    me = lax.axis_index("seq")
    plane, member = lax.div(me, members), lax.rem(me, members)
    wide = 2 * head_width
    span = members * piece
    scale = 1.0 / math.sqrt(head_width)
    has_up, has_down = plane < planes - 1, plane > 0

    def at(peer):
        return {"device_id": (side, peer), "device_id_type": pl.DeviceIdType.MESH}

    def beside(step):
        return at(plane * members + lax.rem(member + step, members))

    above, below = at(me + members), at(me - members)
    across = {"device_id": (1 - side, me), "device_id_type": pl.DeviceIdType.MESH}

    barrier = pltpu.get_barrier_semaphore()
    for step in range(1, members):
        pl.semaphore_signal(barrier, inc=1, **beside(step))
    pl.semaphore_signal(barrier, inc=1, **across)

    @pl.when(has_up)
    def _():
        pl.semaphore_signal(barrier, inc=1, **above)

    @pl.when(has_down)
    def _():
        pl.semaphore_signal(barrier, inc=1, **below)

    pl.semaphore_wait(barrier, members + jnp.where(has_up, 1, 0) + jnp.where(has_down, 1, 0))

    def weight_copy(shard, source, way, target):
        return pltpu.make_async_remote_copy(
            src_ref=source,
            dst_ref=weights.at[shard],
            send_sem=wsend_sem.at[way, shard],
            recv_sem=wrecv_sem.at[shard],
            **target,
        )

    def input_column(chunk, owner):
        return pl.ds(pl.multiple_of((chunk * members + owner) * wide, wide), wide)

    def landing(chunk, index):
        return states.at[chunk, index, :, pl.ds(pl.multiple_of(member * piece, piece), piece), :]

    def send_chunk(chunk, carry):
        for step in range(1, members):
            owner = lax.rem(member + step, members)
            for index, ref in enumerate((q_ref, k_ref, v_ref)):
                pltpu.make_async_remote_copy(
                    src_ref=ref.at[0, :, :, input_column(chunk, owner)],
                    dst_ref=landing(chunk, index),
                    send_sem=send_sem.at[chunk],
                    recv_sem=recv_sem.at[chunk],
                    **beside(step),
                ).start()
        for index, ref in enumerate((q_ref, k_ref, v_ref)):
            pltpu.make_async_copy(
                ref.at[0, :, :, input_column(chunk, member)], landing(chunk, index), local_sem.at[chunk]
            ).start()
        return carry

    lax.fori_loop(0, chunks, send_chunk, 0)

    @pl.when(has_up)
    def _():
        weight_copy(plane, weight_ref, 0, above).start()

    @pl.when(has_down)
    def _():
        weight_copy(plane, weight_ref, 1, below).start()

    own_weights = pltpu.make_async_copy(weight_ref, weights.at[plane], wlocal_sem)
    own_weights.start()

    def relay_weights(step):
        @pl.when(plane - step >= 0)
        def _():
            shard = weights.at[plane - step]
            pltpu.make_async_copy(shard, shard, wrecv_sem.at[plane - step]).wait()

            @pl.when(has_up)
            def _():
                weight_copy(plane - step, shard, 0, above).start()

        @pl.when(plane + step < planes)
        def _():
            shard = weights.at[plane + step]
            pltpu.make_async_copy(shard, shard, wrecv_sem.at[plane + step]).wait()

            @pl.when(has_down)
            def _():
                weight_copy(plane + step, shard, 1, below).start()

    @pl.when(jnp.logical_not(has_up))
    def _():
        queries_up[...] = jnp.zeros_like(queries_up)

    @pl.when(jnp.logical_not(has_down))
    def _():
        up_into[...] = jnp.zeros_like(up_into)
        up_stats_into[...] = jnp.zeros_like(up_stats_into)

    gets_down = jnp.logical_and(has_up, side == 1)
    gives_down = jnp.logical_and(has_down, side == 1)

    @pl.when(jnp.logical_not(gets_down))
    def _():
        down_into[...] = jnp.zeros_like(down_into)
        down_stats_into[...] = jnp.zeros_like(down_stats_into)

    def tables(row, carry):
        table = table_ref[row]
        k_places = lax.broadcasted_iota(jnp.int32, (span, span), 1)
        q_places = lax.broadcasted_iota(jnp.int32, (span, span), 0)
        places = lax.broadcasted_iota(jnp.int32, (span, 2 * span), 1)
        allowed = (k_places >= table[:, 0:1]) & (k_places <= q_places)
        own_bias[row] = jnp.where(allowed, jnp.float32(0), jnp.float32(-1e30))
        up_bias[row] = jnp.where(k_places >= table[:, 1:2], jnp.float32(0), jnp.float32(-1e30))
        own_moves[row] = jnp.where(places == table[:, 2:3], 1.0, 0.0).astype(jnp.bfloat16)
        up_moves[row] = jnp.where(places == table[:, 3:4], 1.0, 0.0).astype(jnp.bfloat16)
        down_moves[row] = jnp.where(k_places == table[:, 4:5], 1.0, 0.0).astype(jnp.bfloat16)
        return carry

    lax.fori_loop(0, rows, tables, 0)

    def attend(chunk, part, q_of, bias_ref):
        def attend_row(row, inner):
            lane = lax.broadcasted_iota(jnp.int32, (span, head_width), 1) - row * 8
            stats = jnp.where(lane == 6, jnp.float32(1), jnp.float32(0))
            for head in range(2):
                lanes = slice(head * head_width, (head + 1) * head_width)
                scores = lax.dot_general(
                    q_of(row, lanes),
                    states[chunk, 1, row, :, lanes],
                    (((1,), (1,)), ((), ())),
                    preferred_element_type=jnp.float32,
                )
                scores = scores * scale + bias_ref[row]
                top = jnp.max(scores, axis=1, keepdims=True)
                raised = jnp.exp(scores - top)
                total = jnp.sum(raised, axis=1, keepdims=True)
                raw[chunk, row, part * span : (part + 1) * span, lanes] = jnp.dot(
                    (raised * (1.0 / total)).astype(jnp.bfloat16),
                    states[chunk, 2, row, :, lanes],
                    preferred_element_type=jnp.float32,
                ).astype(jnp.bfloat16)
                level = top + jnp.log(total)
                for digit in range(3):
                    rounded = level.astype(jnp.bfloat16).astype(jnp.float32)
                    stats = jnp.where(lane == head * 3 + digit, rounded, stats)
                    level = level - rounded
            raw[chunk, row, part * span : (part + 1) * span, wide:] = stats.astype(jnp.bfloat16)
            return inner

        lax.fori_loop(0, rows, attend_row, 0)

    def query_copy(chunk):
        return pltpu.make_async_remote_copy(
            src_ref=states.at[chunk, 0],
            dst_ref=queries_up.at[chunk],
            send_sem=qsend_sem.at[chunk],
            recv_sem=qrecv_sem.at[chunk],
            **below,
        )

    def context_copies(chunk, sources, targets, sends, receives, device):
        return [
            pltpu.make_async_remote_copy(
                src_ref=source.at[chunk],
                dst_ref=target.at[chunk],
                send_sem=sends.at[chunk, index],
                recv_sem=receives.at[chunk, index],
                **device,
            )
            for index, (source, target) in enumerate(zip(sources, targets))
        ]

    def up_copies(chunk):
        return context_copies(
            chunk, (up_from, up_stats_from), (up_into, up_stats_into), usend_sem, urecv_sem, above
        )

    def down_copies(chunk):
        return context_copies(
            chunk, (down_from, down_stats_from), (down_into, down_stats_into), dsend_sem, drecv_sem, below
        )

    def wait_for(refs, sems, chunk):
        for index, ref in enumerate(refs):
            pltpu.make_async_copy(ref.at[chunk], ref.at[chunk], sems.at[chunk, index]).wait()

    def exchange(chunk, head):
        column = pl.multiple_of((2 * head + side) * head_width, head_width)
        there = feats.at[chunk, :, :, pl.ds(column, head_width)]
        return pltpu.make_async_remote_copy(
            src_ref=there,
            dst_ref=there,
            send_sem=csend_sem.at[chunk, head],
            recv_sem=crecv_sem.at[chunk, head],
            **across,
        )

    def local_stage(chunk):
        others = states.at[chunk, :, :, pl.ds(0, span - piece), :]
        pltpu.make_async_copy(others, others, recv_sem.at[chunk]).wait()
        mine = states.at[chunk, :, :, pl.ds(0, piece), :]
        pltpu.make_async_copy(mine, mine, local_sem.at[chunk]).wait()

        @pl.when(has_down)
        def _():
            query_copy(chunk).start()

        attend(chunk, 0, lambda row, lanes: states[chunk, 0, row, :, lanes], own_bias)

    def moved_part(moves, source, chunk, row, target):
        moved = jnp.dot(moves[row], source, preferred_element_type=jnp.float32)
        target[chunk, row] = moved[:, :wide].astype(jnp.bfloat16)
        return moved[:, wide:]

    def cross_stage(chunk):
        @pl.when(has_up)
        def _():
            pltpu.make_async_copy(
                queries_up.at[chunk], queries_up.at[chunk], qrecv_sem.at[chunk]
            ).wait()

        attend(chunk, 1, lambda row, lanes: queries_up[chunk, row, :, lanes], up_bias)

        @pl.when(has_up)
        def _():
            stats = 0.0
            for row in range(rows):
                stats = stats + moved_part(up_moves, raw[chunk, row], chunk, row, up_from)
            up_stats_from[chunk] = stats.astype(jnp.bfloat16)
            for copy in up_copies(chunk):
                copy.start()

        @pl.when(gives_down)
        def _():
            stats = 0.0
            for row in range(rows):
                stats = stats + moved_part(down_moves, raw[chunk, row, :span], chunk, row, down_from)
            down_stats_from[chunk] = stats.astype(jnp.bfloat16)
            for copy in down_copies(chunk):
                copy.start()

        stats = 0.0
        for row in range(rows):
            stats = stats + moved_part(own_moves, raw[chunk, row], chunk, row, own)
        own_stats[chunk] = stats.astype(jnp.bfloat16)

    def merge_stage(chunk):
        @pl.when(has_down)
        def _():
            wait_for((up_into, up_stats_into), urecv_sem, chunk)

        @pl.when(gets_down)
        def _():
            wait_for((down_into, down_stats_into), drecv_sem, chunk)

        for row in range(rows):
            parts = (own, up_into, down_into)
            stats = [
                ref[chunk].astype(jnp.float32)[:, row * 8 : row * 8 + 8]
                for ref in (own_stats, up_stats_into, down_stats_into)
            ]
            for head in range(2):
                lanes = slice(head * head_width, (head + 1) * head_width)
                levels = []
                for stat in stats:
                    level = stat[:, head * 3 : head * 3 + 1] + stat[:, head * 3 + 1 : head * 3 + 2]
                    level = level + stat[:, head * 3 + 2 : head * 3 + 3]
                    levels.append(jnp.where(stat[:, 6:7] > 0.5, level, jnp.float32(-3e30)))
                top = jnp.maximum(jnp.maximum(levels[0], levels[1]), levels[2])
                shares = [jnp.exp(level - top) for level in levels]
                norm = 1.0 / (shares[0] + shares[1] + shares[2])
                value = 0.0
                for part, share in zip(parts, shares):
                    value = value + part[chunk, row, :, lanes].astype(jnp.float32) * (share * norm)
                value = value.astype(jnp.bfloat16)
                column = pl.multiple_of((2 * head + side) * head_width, head_width)
                for owner in range(members):
                    feats[chunk, owner, row * piece : (row + 1) * piece, pl.ds(column, head_width)] = value[
                        owner * piece : (owner + 1) * piece
                    ]
        for head in range(2):
            exchange(chunk, head).start()

    def stage(step, carry):
        @pl.when(step < chunks)
        def _():
            local_stage(step)

        @pl.when(jnp.logical_and(step >= 1, step <= chunks))
        def _():
            cross_stage(step - 1)

        @pl.when(step >= 2)
        def _():
            merge_stage(step - 2)

        for late in range(1, planes - 1):

            @pl.when(step == 2 * late)
            def _():
                relay_weights(late)

        return carry

    lax.fori_loop(0, chunks + 2, stage, 0)

    own_weights.wait()

    def arrive(chunk, carry):
        for head in range(2):
            column = pl.multiple_of((2 * head + 1 - side) * head_width, head_width)
            there = feats.at[chunk, :, :, pl.ds(column, head_width)]
            pltpu.make_async_copy(there, there, crecv_sem.at[chunk, head]).wait()
        return carry

    lax.fori_loop(0, chunks, arrive, 0)

    low_half = plane < planes // 2
    last = jnp.where(low_half, chunks - 1, 0)

    def join_early(owner, carry):
        total = 0.0
        for step in range(chunks - 1):
            chunk = jnp.where(low_half, step, chunks - 1 - step)
            total = total + jnp.dot(
                feats[chunk, owner], weights[chunk], preferred_element_type=jnp.float32
            )
        sums[owner] = total
        return carry

    lax.fori_loop(0, members, join_early, 0)
    relay_weights(planes - 1)

    def partial_copy(owner):
        return pltpu.make_async_remote_copy(
            src_ref=partials.at[owner],
            dst_ref=arrived.at[member],
            send_sem=psend_sem,
            recv_sem=precv_sem,
            **at(plane * members + owner),
        )

    def join_last(step, carry):
        owner = lax.rem(member + 1 + step, members)
        total = sums[owner] + jnp.dot(
            feats[last, owner], weights[last], preferred_element_type=jnp.float32
        )
        partials[owner] = total.astype(jnp.bfloat16)

        @pl.when(step < members - 1)
        def _():
            partial_copy(owner).start()

        return carry

    lax.fori_loop(0, members, join_last, 0)
    arrived[member] = partials[member]
    incoming = arrived.at[pl.ds(0, members - 1)]
    pltpu.make_async_copy(incoming, incoming, precv_sem).wait()
    columns = out_ref.shape[2]
    for row in range(rows):
        total = 0.0
        for source in range(members):
            total = total + arrived[source, row * piece : (row + 1) * piece, :].astype(jnp.float32)
        gate, up = total[:, :columns], total[:, columns:]
        out_ref[row] = (gate / (1.0 + jnp.exp(-gate)) * up).astype(jnp.bfloat16)

    def finish(chunk, carry):
        others = states.at[chunk, :, :, pl.ds(0, span - piece), :]
        pltpu.make_async_copy(others, others, send_sem.at[chunk]).wait()
        for head in range(2):
            exchange(chunk, head).wait_send()

        @pl.when(has_up)
        def _():
            for copy in up_copies(chunk):
                copy.wait_send()

        @pl.when(has_down)
        def _():
            query_copy(chunk).wait_send()

        @pl.when(gives_down)
        def _():
            for copy in down_copies(chunk):
                copy.wait_send()

        return carry

    lax.fori_loop(0, chunks, finish, 0)
    for step in range(planes):

        @pl.when(jnp.logical_and(has_up, plane - step >= 0))
        def _():
            weight_copy(plane - step, weights.at[plane - step], 0, above).wait_send()

        @pl.when(jnp.logical_and(has_down, plane + step < planes))
        def _():
            weight_copy(plane + step, weights.at[plane + step], 1, below).wait_send()

    pltpu.make_async_copy(incoming, incoming, psend_sem).wait()


def fused_body(queries, key_states, value_vectors, hypothesis_lengths, join_weight):
    rows, piece, width = (queries.shape[1], queries.shape[2], queries.shape[3])
    devices = lax.axis_size("seq")
    planes, members = devices // PACKED_ROWS, PACKED_ROWS
    head_width = width // ATTENTION_HEADS
    wide = 2 * head_width
    chunks = width // (members * wide)
    span = members * piece
    row_len = devices * piece
    weight_rows, _, columns = join_weight.shape
    first, mirror = jax.vmap(lambda lengths: hypothesis_tables(lengths, row_len))(hypothesis_lengths)
    places = jnp.broadcast_to(jnp.arange(row_len, dtype=jnp.int32), first.shape)
    leading = lax.axis_index("dir") == 0
    base = lax.axis_index("seq") // members * span

    def part(values, shift, absent):
        padded = jnp.pad(values, ((0, 0), (span, span)), constant_values=absent)
        return lax.dynamic_slice_in_dim(padded, base + span + shift, span, 1) - base

    far = 4 * row_len
    source = jnp.where(leading, places, mirror)
    table = jnp.stack(
        [
            part(first, 0, far),
            part(first, span, far),
            part(source, 0, far),
            part(jnp.where(leading, places, mirror), span, far),
            part(jnp.where(leading, far, mirror), -span, far),
        ]
        + [jnp.zeros((rows, span), jnp.int32)] * 3,
        axis=2,
    )
    geometry = (planes, rows, members, piece, head_width, chunks)

    def vmem(*shape):
        return pltpu.VMEM(shape, jnp.bfloat16)

    dma = pltpu.SemaphoreType.DMA
    context = (chunks, rows, span, wide)
    stats = (chunks, span, head_width)
    return pl.pallas_call(
        functools.partial(pair_kernel, geometry),
        out_shape=jax.ShapeDtypeStruct((rows, piece, columns), jnp.bfloat16),
        in_specs=[pl.BlockSpec(memory_space=pltpu.VMEM)] + [pl.BlockSpec(memory_space=pl.ANY)] * 4,
        out_specs=pl.BlockSpec(memory_space=pltpu.VMEM),
        scratch_shapes=[
            vmem(chunks, 3, rows, span, wide),
            vmem(*context),
            vmem(chunks, rows, 2 * span, wide + head_width),
            *[vmem(*context)] * 5,
            *[vmem(*stats)] * 5,
            vmem(planes, weight_rows, 2 * columns),
            vmem(chunks, members, rows * piece, 2 * wide),
            pltpu.VMEM((members, rows * piece, 2 * columns), jnp.float32),
            vmem(members, rows * piece, 2 * columns),
            vmem(members, rows * piece, 2 * columns),
            vmem(rows, span, 2 * span),
            vmem(rows, span, 2 * span),
            vmem(rows, span, span),
            pltpu.VMEM((rows, span, span), jnp.float32),
            pltpu.VMEM((rows, span, span), jnp.float32),
            dma((chunks,)),
            dma((chunks,)),
            dma((chunks,)),
            dma((chunks,)),
            dma((chunks,)),
            dma((chunks, 2)),
            dma((chunks, 2)),
            dma((chunks, 2)),
            dma((chunks, 2)),
            dma((2, planes)),
            dma((planes,)),
            dma,
            dma((chunks, 2)),
            dma((chunks, 2)),
            dma,
            dma,
        ],
        compiler_params=pltpu.CompilerParams(
            collective_id=0, has_side_effects=True, vmem_limit_bytes=60 * 1024 * 1024
        ),
    )(
        table,
        queries,
        key_states,
        value_vectors,
        join_weight.reshape(weight_rows, 2 * columns),
    )


def fits_kernel(mesh):
    planes = mesh.shape["seq"] // PACKED_ROWS
    return ATTENTION_HEADS // planes == 2 * PACKED_ROWS


def solution(mesh):
    return jax.shard_map(
        fused_body if fits_kernel(mesh) else body,
        mesh=mesh,
        in_specs=(
            P("dir", None, "seq", None),
            P("dir", None, "seq", None),
            P("dir", None, "seq", None),
            P(),
            P("seq", None, "dir"),
        ),
        out_specs=P(None, "seq", "dir"),
        check_vma=False,
    )
```

```python
import functools
import math

import jax
import jax.numpy as jnp
from jax import lax
from jax.experimental import pallas as pl
from jax.experimental.pallas import tpu as pltpu
from jax.sharding import PartitionSpec as P

ATTENTION_HEADS = 32
LONGEST_TOKENS = 256
PACKED_ROWS = 4


def swapped(array, axis, stride):
    return lax.ppermute(array, axis, [(i, i ^ 1 << stride) for i in range(lax.axis_size(axis))])


def hypothesis_tables(length_list, row_len):
    ends = jnp.cumsum(length_list)
    starts = ends - length_list
    places = jnp.arange(row_len, dtype=jnp.int32)
    inside = (places[:, None] >= starts[None, :]) & (places[:, None] < ends[None, :])
    first = jnp.sum(jnp.where(inside, starts[None, :], 0), axis=1)
    after = jnp.sum(jnp.where(inside, ends[None, :], 0), axis=1)
    mirror = first + after - 1 - places
    return (first, mirror)


def attend_group(query_row, k_row, v_row, first):
    row_len = query_row.shape[0]
    block_item = min(512, row_len)
    token_span = min(block_item + LONGEST_TOKENS, row_len)
    scale = 1.0 / math.sqrt(query_row.shape[2])

    def single_block(index):
        q_start = index * block_item
        k_start = jnp.maximum(q_start + block_item - token_span, 0)
        q_part = lax.dynamic_slice_in_dim(query_row, q_start, block_item, 0)
        k_part = lax.dynamic_slice_in_dim(k_row, k_start, token_span, 0)
        v_part = lax.dynamic_slice_in_dim(v_row, k_start, token_span, 0)
        scores = (
            jnp.einsum("qhc,khc->hqk", q_part, k_part, preferred_element_type=jnp.float32) * scale
        )
        q_places = q_start + jnp.arange(block_item, dtype=jnp.int32)
        k_places = k_start + jnp.arange(token_span, dtype=jnp.int32)
        starts = lax.dynamic_slice_in_dim(first, q_start, block_item, 0)
        allowed = (k_places[None, :] >= starts[:, None]) & (k_places[None, :] <= q_places[:, None])
        scores = jnp.where(allowed[None], scores, jnp.float32(-1e30))
        top = jnp.max(scores, axis=2, keepdims=True)
        raised = jnp.exp(scores - top)
        weights = (raised / jnp.sum(raised, axis=2, keepdims=True)).astype(jnp.bfloat16)
        return jnp.einsum(
            "hqk,khc->qhc", weights, v_part, preferred_element_type=jnp.float32
        ).astype(jnp.bfloat16)

    block_list = lax.map(single_block, jnp.arange(row_len // block_item, dtype=jnp.int32))
    return block_list.reshape(row_len, query_row.shape[1], query_row.shape[2])


def body(queries, key_states, value_vectors, hypothesis_lengths, join_weight):
    rows, piece, width = (queries.shape[1], queries.shape[2], queries.shape[3])
    devices = lax.axis_size("seq")
    groups = devices // rows
    head_width = width // ATTENTION_HEADS
    pair = width // groups
    heads_here = pair // head_width
    row_bits = rows.bit_length() - 1
    place = lax.axis_index("seq")
    row = place % rows
    row_len = devices * piece

    def regroup(states):
        states = states.reshape(rows, piece, groups, pair)
        return jnp.transpose(states, (2, 0, 1, 3)).reshape(groups * rows, piece, pair)

    q_all, k_all, v_all = (
        lax.all_to_all(regroup(queries[0]), "seq", split_axis=0, concat_axis=1, tiled=True),
        lax.all_to_all(regroup(key_states[0]), "seq", split_axis=0, concat_axis=1, tiled=True),
        lax.all_to_all(regroup(value_vectors[0]), "seq", split_axis=0, concat_axis=1, tiled=True),
    )
    block_rows = join_weight
    for bit in range(row_bits):
        partner = swapped(block_rows, "seq", bit)
        lower = place // 2**bit % 2 == 0
        block_rows = jnp.where(
            lower,
            jnp.concatenate([block_rows, partner], 0),
            jnp.concatenate([partner, block_rows], 0),
        )
    length_list = lax.dynamic_index_in_dim(hypothesis_lengths, row, 0, keepdims=False)
    first, mirror = hypothesis_tables(length_list, row_len)
    array_shape = (row_len, heads_here, head_width)
    context_vectors = attend_group(
        q_all.reshape(array_shape), k_all.reshape(array_shape), v_all.reshape(array_shape), first
    )
    other = swapped(context_vectors, "dir", 0)
    side = lax.axis_index("dir")
    left_side = jnp.where(side == 0, context_vectors, other)
    right_side = jnp.where(side == 0, other, context_vectors)
    right_side = jnp.take(right_side, mirror, axis=0)
    feature_rows = jnp.stack([left_side, right_side], axis=2).reshape(row_len, 2 * pair)
    columns = block_rows.shape[2]
    partial_value = jnp.dot(
        feature_rows, block_rows.reshape(2 * pair, 2 * columns), preferred_element_type=jnp.float32
    ).astype(jnp.bfloat16)
    arrived = lax.all_to_all(
        partial_value.reshape(devices, piece, 2 * columns),
        "seq",
        split_axis=0,
        concat_axis=0,
        tiled=True,
    )
    totals = jnp.sum(arrived.reshape(groups, rows, piece, 2 * columns).astype(jnp.float32), axis=0)
    joined = jax.nn.silu(totals[..., :columns]) * totals[..., columns:]
    return joined.astype(jnp.bfloat16)


def pair_kernel(
    geometry, lengths_ref, q_ref, k_ref, v_ref, weight_ref, out_ref,
    states, queries_up, raw, own, up_from, up_into, down_from, down_into,
    own_stats, up_stats_from, up_stats_into, down_stats_from, down_stats_into,
    weights, feats, sums, partials, arrived, own_moves, up_moves, down_moves, own_bias, up_bias,
    send_sem, recv_sem, local_sem, qsend_sem, qrecv_sem, usend_sem, urecv_sem, dsend_sem, drecv_sem,
    wsend_sem, wrecv_sem, wlocal_sem, csend_sem, crecv_sem, psend_sem, precv_sem,
):
    planes, rows, members, piece, head_width, chunks, halves = geometry
    side = lax.axis_index("dir")
    me = lax.axis_index("seq")
    plane, member = lax.div(me, members), lax.rem(me, members)
    wide = 2 * head_width
    span = members * piece
    scale = 1.0 / math.sqrt(head_width)
    has_up, has_down = plane < planes - 1, plane > 0

    def at(peer):
        return {"device_id": (side, peer), "device_id_type": pl.DeviceIdType.MESH}

    def beside(step):
        return at(plane * members + lax.rem(member + step, members))

    above, below = at(me + members), at(me - members)
    across = {"device_id": (1 - side, me), "device_id_type": pl.DeviceIdType.MESH}

    barrier = pltpu.get_barrier_semaphore()
    for step in range(1, members):
        pl.semaphore_signal(barrier, inc=1, **beside(step))
    pl.semaphore_signal(barrier, inc=1, **across)

    @pl.when(has_up)
    def _():
        pl.semaphore_signal(barrier, inc=1, **above)

    @pl.when(has_down)
    def _():
        pl.semaphore_signal(barrier, inc=1, **below)

    pl.semaphore_wait(barrier, members + jnp.where(has_up, 1, 0) + jnp.where(has_down, 1, 0))

    def weight_copy(shard, half, source, way, target):
        return pltpu.make_async_remote_copy(
            src_ref=source,
            dst_ref=weights.at[shard, half],
            send_sem=wsend_sem.at[way, shard, half],
            recv_sem=wrecv_sem.at[shard, half],
            **target,
        )

    def input_column(chunk, owner):
        return pl.ds(pl.multiple_of((chunk * members + owner) * wide, wide), wide)

    def landing(chunk, index):
        return states.at[chunk, index, :, pl.ds(pl.multiple_of(member * piece, piece), piece), :]

    def send_chunk(chunk, carry):
        for step in range(1, members):
            owner = lax.rem(member + step, members)
            for index, ref in enumerate((q_ref, k_ref, v_ref)):
                pltpu.make_async_remote_copy(
                    src_ref=ref.at[0, :, :, input_column(chunk, owner)],
                    dst_ref=landing(chunk, index),
                    send_sem=send_sem.at[chunk],
                    recv_sem=recv_sem.at[chunk],
                    **beside(step),
                ).start()
        for index, ref in enumerate((q_ref, k_ref, v_ref)):
            pltpu.make_async_copy(
                ref.at[0, :, :, input_column(chunk, member)], landing(chunk, index), local_sem.at[chunk]
            ).start()
        return carry

    lax.fori_loop(0, chunks, send_chunk, 0)

    @pl.when(has_up)
    def _():
        for half in range(halves):
            weight_copy(plane, half, weight_ref.at[half], 0, above).start()

    @pl.when(has_down)
    def _():
        for half in range(halves):
            weight_copy(plane, half, weight_ref.at[half], 1, below).start()

    own_weights = pltpu.make_async_copy(weight_ref, weights.at[plane], wlocal_sem)
    own_weights.start()

    def relay_weights(step, half):
        @pl.when(plane - step >= 0)
        def _():
            shard = weights.at[plane - step, half]
            pltpu.make_async_copy(shard, shard, wrecv_sem.at[plane - step, half]).wait()

            @pl.when(has_up)
            def _():
                weight_copy(plane - step, half, shard, 0, above).start()

        @pl.when(plane + step < planes)
        def _():
            shard = weights.at[plane + step, half]
            pltpu.make_async_copy(shard, shard, wrecv_sem.at[plane + step, half]).wait()

            @pl.when(has_down)
            def _():
                weight_copy(plane + step, half, shard, 1, below).start()

    @pl.when(jnp.logical_not(has_up))
    def _():
        queries_up[...] = jnp.zeros_like(queries_up)

    @pl.when(jnp.logical_not(has_down))
    def _():
        up_into[...] = jnp.zeros_like(up_into)
        up_stats_into[...] = jnp.zeros_like(up_stats_into)

    gets_down = jnp.logical_and(has_up, side == 1)
    gives_down = jnp.logical_and(has_down, side == 1)

    @pl.when(jnp.logical_not(gets_down))
    def _():
        down_into[...] = jnp.zeros_like(down_into)
        down_stats_into[...] = jnp.zeros_like(down_stats_into)

    slots = lengths_ref.shape[1]
    before = lax.broadcasted_iota(jnp.int32, (slots, slots), 0)
    after = lax.broadcasted_iota(jnp.int32, (slots, slots), 1)
    lengths = lengths_ref[...].astype(jnp.float32)
    all_ends = jnp.dot(
        lengths.astype(jnp.bfloat16),
        jnp.where(before <= after, 1.0, 0.0).astype(jnp.bfloat16),
        preferred_element_type=jnp.float32,
    )
    base = plane * span
    far = 4 * planes * span

    def places_of(row, shift):
        ends = all_ends[row : row + 1].astype(jnp.int32)
        starts = ends - lengths_ref[row : row + 1]
        wide_places = base + shift + lax.broadcasted_iota(jnp.int32, (span, slots), 0)
        inside = (wide_places >= starts) & (wide_places < ends)
        place = base + shift + lax.broadcasted_iota(jnp.int32, (span, 1), 0)
        first = jnp.sum(jnp.where(inside, starts, 0), axis=1, keepdims=True)
        last = jnp.sum(jnp.where(inside, ends, 0), axis=1, keepdims=True) - 1
        return first - base, place - base, first + last - place - base

    k_places = lax.broadcasted_iota(jnp.int32, (span, span), 1)
    q_places = lax.broadcasted_iota(jnp.int32, (span, span), 0)
    places = lax.broadcasted_iota(jnp.int32, (span, 2 * span), 1)
    for row in range(rows):
        first, place, mirror = places_of(row, 0)
        allowed = (k_places >= first) & (k_places <= q_places)
        own_bias[row] = jnp.where(allowed, jnp.float32(0), jnp.float32(-1e30))
        source = jnp.where(side == 0, place, mirror)
        own_moves[row] = jnp.where(places == source, 1.0, 0.0).astype(jnp.bfloat16)
        first, place, mirror = places_of(row, span)
        first = jnp.where(has_up, first, far)
        up_bias[row] = jnp.where(k_places >= first, jnp.float32(0), jnp.float32(-1e30))
        source = jnp.where(side == 0, place, mirror)
        up_moves[row] = jnp.where(places == source, 1.0, 0.0).astype(jnp.bfloat16)
        first, place, mirror = places_of(row, -span)
        source = jnp.where(gives_down, mirror, far)
        down_moves[row] = jnp.where(k_places == source, 1.0, 0.0).astype(jnp.bfloat16)

    def attend(chunk, part, q_of, bias_ref):
        def attend_row(row, inner):
            lane = lax.broadcasted_iota(jnp.int32, (span, head_width), 1) - row * 8
            stats = jnp.where(lane == 6, jnp.float32(1), jnp.float32(0))
            for head in range(2):
                lanes = slice(head * head_width, (head + 1) * head_width)
                scores = lax.dot_general(
                    q_of(row, lanes),
                    states[chunk, 1, row, :, lanes],
                    (((1,), (1,)), ((), ())),
                    preferred_element_type=jnp.float32,
                )
                scores = scores * scale + bias_ref[row]
                top = jnp.max(scores, axis=1, keepdims=True)
                raised = jnp.exp(scores - top)
                total = jnp.sum(raised, axis=1, keepdims=True)
                raw[chunk, row, part * span : (part + 1) * span, lanes] = jnp.dot(
                    (raised * (1.0 / total)).astype(jnp.bfloat16),
                    states[chunk, 2, row, :, lanes],
                    preferred_element_type=jnp.float32,
                ).astype(jnp.bfloat16)
                level = top + jnp.log(total)
                for digit in range(3):
                    rounded = level.astype(jnp.bfloat16).astype(jnp.float32)
                    stats = jnp.where(lane == head * 3 + digit, rounded, stats)
                    level = level - rounded
            raw[chunk, row, part * span : (part + 1) * span, wide:] = stats.astype(jnp.bfloat16)
            return inner

        lax.fori_loop(0, rows, attend_row, 0)

    def query_copy(chunk):
        return pltpu.make_async_remote_copy(
            src_ref=states.at[chunk, 0],
            dst_ref=queries_up.at[chunk],
            send_sem=qsend_sem.at[chunk],
            recv_sem=qrecv_sem.at[chunk],
            **below,
        )

    def context_copies(chunk, sources, targets, sends, receives, device):
        return [
            pltpu.make_async_remote_copy(
                src_ref=source.at[chunk],
                dst_ref=target.at[chunk],
                send_sem=sends.at[chunk, index],
                recv_sem=receives.at[chunk, index],
                **device,
            )
            for index, (source, target) in enumerate(zip(sources, targets))
        ]

    def up_copies(chunk):
        return context_copies(
            chunk, (up_from, up_stats_from), (up_into, up_stats_into), usend_sem, urecv_sem, above
        )

    def down_copies(chunk):
        return context_copies(
            chunk, (down_from, down_stats_from), (down_into, down_stats_into), dsend_sem, drecv_sem, below
        )

    def wait_for(refs, sems, chunk):
        for index, ref in enumerate(refs):
            pltpu.make_async_copy(ref.at[chunk], ref.at[chunk], sems.at[chunk, index]).wait()

    def exchange(chunk, head):
        column = pl.multiple_of((2 * head + side) * head_width, head_width)
        there = feats.at[chunk, :, :, pl.ds(column, head_width)]
        return pltpu.make_async_remote_copy(
            src_ref=there,
            dst_ref=there,
            send_sem=csend_sem.at[chunk, head],
            recv_sem=crecv_sem.at[chunk, head],
            **across,
        )

    def local_stage(chunk):
        others = states.at[chunk, :, :, pl.ds(0, span - piece), :]
        pltpu.make_async_copy(others, others, recv_sem.at[chunk]).wait()
        mine = states.at[chunk, :, :, pl.ds(0, piece), :]
        pltpu.make_async_copy(mine, mine, local_sem.at[chunk]).wait()

        @pl.when(has_down)
        def _():
            query_copy(chunk).start()

        attend(chunk, 0, lambda row, lanes: states[chunk, 0, row, :, lanes], own_bias)

    def moved_part(moves, source, chunk, row, target):
        moved = jnp.dot(moves[row], source, preferred_element_type=jnp.float32)
        target[chunk, row] = moved[:, :wide].astype(jnp.bfloat16)
        return moved[:, wide:]

    def cross_stage(chunk):
        @pl.when(has_up)
        def _():
            pltpu.make_async_copy(
                queries_up.at[chunk], queries_up.at[chunk], qrecv_sem.at[chunk]
            ).wait()

        attend(chunk, 1, lambda row, lanes: queries_up[chunk, row, :, lanes], up_bias)

        @pl.when(has_up)
        def _():
            stats = 0.0
            for row in range(rows):
                stats = stats + moved_part(up_moves, raw[chunk, row], chunk, row, up_from)
            up_stats_from[chunk] = stats.astype(jnp.bfloat16)
            for copy in up_copies(chunk):
                copy.start()

        @pl.when(gives_down)
        def _():
            stats = 0.0
            for row in range(rows):
                stats = stats + moved_part(down_moves, raw[chunk, row, :span], chunk, row, down_from)
            down_stats_from[chunk] = stats.astype(jnp.bfloat16)
            for copy in down_copies(chunk):
                copy.start()

        stats = 0.0
        for row in range(rows):
            stats = stats + moved_part(own_moves, raw[chunk, row], chunk, row, own)
        own_stats[chunk] = stats.astype(jnp.bfloat16)

    def merge_stage(chunk):
        @pl.when(has_down)
        def _():
            wait_for((up_into, up_stats_into), urecv_sem, chunk)

        @pl.when(gets_down)
        def _():
            wait_for((down_into, down_stats_into), drecv_sem, chunk)

        for row in range(rows):
            parts = (own, up_into, down_into)
            stats = [
                ref[chunk].astype(jnp.float32)[:, row * 8 : row * 8 + 8]
                for ref in (own_stats, up_stats_into, down_stats_into)
            ]
            for head in range(2):
                lanes = slice(head * head_width, (head + 1) * head_width)
                levels = []
                for stat in stats:
                    level = stat[:, head * 3 : head * 3 + 1] + stat[:, head * 3 + 1 : head * 3 + 2]
                    level = level + stat[:, head * 3 + 2 : head * 3 + 3]
                    levels.append(jnp.where(stat[:, 6:7] > 0.5, level, jnp.float32(-3e30)))
                top = jnp.maximum(jnp.maximum(levels[0], levels[1]), levels[2])
                shares = [jnp.exp(level - top) for level in levels]
                norm = 1.0 / (shares[0] + shares[1] + shares[2])
                value = 0.0
                for part, share in zip(parts, shares):
                    value = value + part[chunk, row, :, lanes].astype(jnp.float32) * (share * norm)
                value = value.astype(jnp.bfloat16)
                column = pl.multiple_of((2 * head + side) * head_width, head_width)
                for owner in range(members):
                    feats[chunk, owner, row * piece : (row + 1) * piece, pl.ds(column, head_width)] = value[
                        owner * piece : (owner + 1) * piece
                    ]
        for head in range(2):
            exchange(chunk, head).start()

    def stage(step, carry):
        @pl.when(step < chunks)
        def _():
            local_stage(step)

        for late in range(1, planes - 1):

            @pl.when(step == late)
            def _():
                for half in range(halves):
                    relay_weights(late, half)

        @pl.when(jnp.logical_and(step >= 1, step <= chunks))
        def _():
            cross_stage(step - 1)

        @pl.when(step >= 2)
        def _():
            merge_stage(step - 2)

        return carry

    lax.fori_loop(0, chunks + 2, stage, 0)

    own_weights.wait()

    def arrive(chunk, carry):
        for head in range(2):
            column = pl.multiple_of((2 * head + 1 - side) * head_width, head_width)
            there = feats.at[chunk, :, :, pl.ds(column, head_width)]
            pltpu.make_async_copy(there, there, crecv_sem.at[chunk, head]).wait()
        return carry

    lax.fori_loop(0, chunks, arrive, 0)

    low_half = plane < planes // 2
    last = jnp.where(low_half, chunks - 1, 0)

    def join_early(owner, carry):
        for half in range(halves):
            total = 0.0
            for step in range(chunks - 1):
                chunk = jnp.where(low_half, step, chunks - 1 - step)
                total = total + jnp.dot(
                    feats[chunk, owner], weights[chunk, half], preferred_element_type=jnp.float32
                )
            sums[half, owner] = total
        return carry

    lax.fori_loop(0, members, join_early, 0)

    def partial_copy(half, owner):
        return pltpu.make_async_remote_copy(
            src_ref=partials.at[half, owner],
            dst_ref=arrived.at[half, member],
            send_sem=psend_sem.at[half],
            recv_sem=precv_sem.at[half],
            **at(plane * members + owner),
        )

    def join_half(half, carry):
        relay_weights(planes - 1, half)

        def join_last(step, inner):
            owner = lax.rem(member + 1 + step, members)
            total = sums[half, owner] + jnp.dot(
                feats[last, owner], weights[last, half], preferred_element_type=jnp.float32
            )
            partials[half, owner] = total.astype(jnp.bfloat16)

            @pl.when(step < members - 1)
            def _():
                partial_copy(half, owner).start()

            return inner

        lax.fori_loop(0, members, join_last, 0)
        arrived[half, member] = partials[half, member]
        return carry

    lax.fori_loop(0, halves, join_half, 0)
    columns = out_ref.shape[2] // halves
    for half in range(halves):
        incoming = arrived.at[half, pl.ds(0, members - 1)]
        pltpu.make_async_copy(incoming, incoming, precv_sem.at[half]).wait()
        for row in range(rows):
            total = 0.0
            for source in range(members):
                total = total + arrived[half, source, row * piece : (row + 1) * piece, :].astype(
                    jnp.float32
                )
            gate, up = total[:, :columns], total[:, columns:]
            out_ref[row, :, half * columns : (half + 1) * columns] = (
                gate / (1.0 + jnp.exp(-gate)) * up
            ).astype(jnp.bfloat16)

    def finish(chunk, carry):
        others = states.at[chunk, :, :, pl.ds(0, span - piece), :]
        pltpu.make_async_copy(others, others, send_sem.at[chunk]).wait()
        for head in range(2):
            exchange(chunk, head).wait_send()

        @pl.when(has_up)
        def _():
            for copy in up_copies(chunk):
                copy.wait_send()

        @pl.when(has_down)
        def _():
            query_copy(chunk).wait_send()

        @pl.when(gives_down)
        def _():
            for copy in down_copies(chunk):
                copy.wait_send()

        return carry

    lax.fori_loop(0, chunks, finish, 0)
    for step in range(planes):

        @pl.when(jnp.logical_and(has_up, plane - step >= 0))
        def _():
            for half in range(halves):
                weight_copy(plane - step, half, weights.at[plane - step, half], 0, above).wait_send()

        @pl.when(jnp.logical_and(has_down, plane + step < planes))
        def _():
            for half in range(halves):
                weight_copy(plane + step, half, weights.at[plane + step, half], 1, below).wait_send()

    for half in range(halves):
        incoming = arrived.at[half, pl.ds(0, members - 1)]
        pltpu.make_async_copy(incoming, incoming, psend_sem.at[half]).wait()


def fused_body(queries, key_states, value_vectors, hypothesis_lengths, join_weight):
    rows, piece, width = (queries.shape[1], queries.shape[2], queries.shape[3])
    devices = lax.axis_size("seq")
    planes, members = devices // PACKED_ROWS, PACKED_ROWS
    head_width = width // ATTENTION_HEADS
    wide = 2 * head_width
    chunks = width // (members * wide)
    span = members * piece
    halves = 2
    weight_rows, _, columns = join_weight.shape
    part = columns // halves
    by_halves = jnp.transpose(join_weight.reshape(weight_rows, 2, halves, part), (2, 0, 1, 3))
    geometry = (planes, rows, members, piece, head_width, chunks, halves)

    def vmem(*shape):
        return pltpu.VMEM(shape, jnp.bfloat16)

    dma = pltpu.SemaphoreType.DMA
    context = (chunks, rows, span, wide)
    stats = (chunks, span, head_width)
    return pl.pallas_call(
        functools.partial(pair_kernel, geometry),
        out_shape=jax.ShapeDtypeStruct((rows, piece, columns), jnp.bfloat16),
        in_specs=[pl.BlockSpec(memory_space=pltpu.VMEM)] + [pl.BlockSpec(memory_space=pl.ANY)] * 4,
        out_specs=pl.BlockSpec(memory_space=pltpu.VMEM),
        scratch_shapes=[
            vmem(chunks, 3, rows, span, wide),
            vmem(*context),
            vmem(chunks, rows, 2 * span, wide + head_width),
            *[vmem(*context)] * 5,
            *[vmem(*stats)] * 5,
            vmem(planes, halves, weight_rows, 2 * part),
            vmem(chunks, members, rows * piece, 2 * wide),
            pltpu.VMEM((halves, members, rows * piece, 2 * part), jnp.float32),
            vmem(halves, members, rows * piece, 2 * part),
            vmem(halves, members, rows * piece, 2 * part),
            vmem(rows, span, 2 * span),
            vmem(rows, span, 2 * span),
            vmem(rows, span, span),
            pltpu.VMEM((rows, span, span), jnp.float32),
            pltpu.VMEM((rows, span, span), jnp.float32),
            dma((chunks,)),
            dma((chunks,)),
            dma((chunks,)),
            dma((chunks,)),
            dma((chunks,)),
            dma((chunks, 2)),
            dma((chunks, 2)),
            dma((chunks, 2)),
            dma((chunks, 2)),
            dma((2, planes, halves)),
            dma((planes, halves)),
            dma,
            dma((chunks, 2)),
            dma((chunks, 2)),
            dma((halves,)),
            dma((halves,)),
        ],
        compiler_params=pltpu.CompilerParams(
            collective_id=0, has_side_effects=True, vmem_limit_bytes=60 * 1024 * 1024
        ),
    )(
        hypothesis_lengths,
        queries,
        key_states,
        value_vectors,
        by_halves.reshape(halves, weight_rows, 2 * part),
    )


def fits_kernel(mesh):
    planes = mesh.shape["seq"] // PACKED_ROWS
    return ATTENTION_HEADS // planes == 2 * PACKED_ROWS


def solution(mesh):
    return jax.shard_map(
        fused_body if fits_kernel(mesh) else body,
        mesh=mesh,
        in_specs=(
            P("dir", None, "seq", None),
            P("dir", None, "seq", None),
            P("dir", None, "seq", None),
            P(),
            P("seq", None, "dir"),
        ),
        out_specs=P(None, "seq", "dir"),
        check_vma=False,
    )
```

```python
import functools
import math

import jax
import jax.numpy as jnp
from jax import lax
from jax.experimental import pallas as pl
from jax.experimental.pallas import tpu as pltpu
from jax.sharding import PartitionSpec as P

ATTENTION_HEADS = 32
LONGEST_TOKENS = 256
PACKED_ROWS = 4


def swapped(array, axis, stride):
    return lax.ppermute(array, axis, [(i, i ^ 1 << stride) for i in range(lax.axis_size(axis))])


def hypothesis_tables(length_list, row_len):
    ends = jnp.cumsum(length_list)
    starts = ends - length_list
    places = jnp.arange(row_len, dtype=jnp.int32)
    inside = (places[:, None] >= starts[None, :]) & (places[:, None] < ends[None, :])
    first = jnp.sum(jnp.where(inside, starts[None, :], 0), axis=1)
    after = jnp.sum(jnp.where(inside, ends[None, :], 0), axis=1)
    mirror = first + after - 1 - places
    return (first, mirror)


def attend_group(query_row, k_row, v_row, first):
    row_len = query_row.shape[0]
    block_item = min(512, row_len)
    token_span = min(block_item + LONGEST_TOKENS, row_len)
    scale = 1.0 / math.sqrt(query_row.shape[2])

    def single_block(index):
        q_start = index * block_item
        k_start = jnp.maximum(q_start + block_item - token_span, 0)
        q_part = lax.dynamic_slice_in_dim(query_row, q_start, block_item, 0)
        k_part = lax.dynamic_slice_in_dim(k_row, k_start, token_span, 0)
        v_part = lax.dynamic_slice_in_dim(v_row, k_start, token_span, 0)
        scores = (
            jnp.einsum("qhc,khc->hqk", q_part, k_part, preferred_element_type=jnp.float32) * scale
        )
        q_places = q_start + jnp.arange(block_item, dtype=jnp.int32)
        k_places = k_start + jnp.arange(token_span, dtype=jnp.int32)
        starts = lax.dynamic_slice_in_dim(first, q_start, block_item, 0)
        allowed = (k_places[None, :] >= starts[:, None]) & (k_places[None, :] <= q_places[:, None])
        scores = jnp.where(allowed[None], scores, jnp.float32(-1e30))
        top = jnp.max(scores, axis=2, keepdims=True)
        raised = jnp.exp(scores - top)
        weights = (raised / jnp.sum(raised, axis=2, keepdims=True)).astype(jnp.bfloat16)
        return jnp.einsum(
            "hqk,khc->qhc", weights, v_part, preferred_element_type=jnp.float32
        ).astype(jnp.bfloat16)

    block_list = lax.map(single_block, jnp.arange(row_len // block_item, dtype=jnp.int32))
    return block_list.reshape(row_len, query_row.shape[1], query_row.shape[2])


def body(queries, key_states, value_vectors, hypothesis_lengths, join_weight):
    rows, piece, width = (queries.shape[1], queries.shape[2], queries.shape[3])
    devices = lax.axis_size("seq")
    groups = devices // rows
    head_width = width // ATTENTION_HEADS
    pair = width // groups
    heads_here = pair // head_width
    row_bits = rows.bit_length() - 1
    place = lax.axis_index("seq")
    row = place % rows
    row_len = devices * piece

    def regroup(states):
        states = states.reshape(rows, piece, groups, pair)
        return jnp.transpose(states, (2, 0, 1, 3)).reshape(groups * rows, piece, pair)

    q_all, k_all, v_all = (
        lax.all_to_all(regroup(queries[0]), "seq", split_axis=0, concat_axis=1, tiled=True),
        lax.all_to_all(regroup(key_states[0]), "seq", split_axis=0, concat_axis=1, tiled=True),
        lax.all_to_all(regroup(value_vectors[0]), "seq", split_axis=0, concat_axis=1, tiled=True),
    )
    block_rows = join_weight
    for bit in range(row_bits):
        partner = swapped(block_rows, "seq", bit)
        lower = place // 2**bit % 2 == 0
        block_rows = jnp.where(
            lower,
            jnp.concatenate([block_rows, partner], 0),
            jnp.concatenate([partner, block_rows], 0),
        )
    length_list = lax.dynamic_index_in_dim(hypothesis_lengths, row, 0, keepdims=False)
    first, mirror = hypothesis_tables(length_list, row_len)
    array_shape = (row_len, heads_here, head_width)
    context_vectors = attend_group(
        q_all.reshape(array_shape), k_all.reshape(array_shape), v_all.reshape(array_shape), first
    )
    other = swapped(context_vectors, "dir", 0)
    side = lax.axis_index("dir")
    left_side = jnp.where(side == 0, context_vectors, other)
    right_side = jnp.where(side == 0, other, context_vectors)
    right_side = jnp.take(right_side, mirror, axis=0)
    feature_rows = jnp.stack([left_side, right_side], axis=2).reshape(row_len, 2 * pair)
    columns = block_rows.shape[2]
    partial_value = jnp.dot(
        feature_rows, block_rows.reshape(2 * pair, 2 * columns), preferred_element_type=jnp.float32
    ).astype(jnp.bfloat16)
    arrived = lax.all_to_all(
        partial_value.reshape(devices, piece, 2 * columns),
        "seq",
        split_axis=0,
        concat_axis=0,
        tiled=True,
    )
    totals = jnp.sum(arrived.reshape(groups, rows, piece, 2 * columns).astype(jnp.float32), axis=0)
    joined = jax.nn.silu(totals[..., :columns]) * totals[..., columns:]
    return joined.astype(jnp.bfloat16)


def pair_kernel(
    geometry, lengths_ref, q_ref, k_ref, v_ref, weight_ref, out_ref,
    states, queries_up, raw, own, up_from, up_into, down_from, down_into,
    own_stats, up_stats_from, up_stats_into, down_stats_from, down_stats_into,
    weights, feats, sums, partials, arrived, own_moves, up_moves, down_moves, own_bias, up_bias,
    send_sem, recv_sem, local_sem, qsend_sem, qrecv_sem, usend_sem, urecv_sem, dsend_sem, drecv_sem,
    wsend_sem, wrecv_sem, wlocal_sem, csend_sem, crecv_sem, psend_sem, precv_sem,
):
    planes, rows, members, piece, head_width, chunks, halves = geometry
    side = lax.axis_index("dir")
    me = lax.axis_index("seq")
    plane, member = lax.div(me, members), lax.rem(me, members)
    wide = 2 * head_width
    span = members * piece
    scale = 1.0 / math.sqrt(head_width)
    has_up, has_down = plane < planes - 1, plane > 0

    def at(peer):
        return {"device_id": (side, peer), "device_id_type": pl.DeviceIdType.MESH}

    def beside(step):
        return at(plane * members + lax.rem(member + step, members))

    above, below = at(me + members), at(me - members)
    across = {"device_id": (1 - side, me), "device_id_type": pl.DeviceIdType.MESH}

    barrier = pltpu.get_barrier_semaphore()
    for step in range(1, members):
        pl.semaphore_signal(barrier, inc=1, **beside(step))
    pl.semaphore_signal(barrier, inc=1, **across)

    @pl.when(has_up)
    def _():
        pl.semaphore_signal(barrier, inc=1, **above)

    @pl.when(has_down)
    def _():
        pl.semaphore_signal(barrier, inc=1, **below)

    pl.semaphore_wait(barrier, members + jnp.where(has_up, 1, 0) + jnp.where(has_down, 1, 0))

    def weight_copy(shard, half, source, way, target):
        return pltpu.make_async_remote_copy(
            src_ref=source,
            dst_ref=weights.at[shard, half],
            send_sem=wsend_sem.at[way, shard, half],
            recv_sem=wrecv_sem.at[shard, half],
            **target,
        )

    def input_column(chunk, owner):
        return pl.ds(pl.multiple_of((chunk * members + owner) * wide, wide), wide)

    def landing(chunk, index):
        return states.at[chunk, index, :, pl.ds(pl.multiple_of(member * piece, piece), piece), :]

    def send_chunk(chunk):
        for step in range(1, members):
            owner = lax.rem(member + step, members)
            for index, ref in enumerate((q_ref, k_ref, v_ref)):
                pltpu.make_async_remote_copy(
                    src_ref=ref.at[0, :, :, input_column(chunk, owner)],
                    dst_ref=landing(chunk, index),
                    send_sem=send_sem.at[chunk],
                    recv_sem=recv_sem.at[chunk],
                    **beside(step),
                ).start()
        for index, ref in enumerate((q_ref, k_ref, v_ref)):
            pltpu.make_async_copy(
                ref.at[0, :, :, input_column(chunk, member)], landing(chunk, index), local_sem.at[chunk]
            ).start()

    def send_own_weights(half):
        @pl.when(has_up)
        def _():
            weight_copy(plane, half, weight_ref.at[half], 0, above).start()

        @pl.when(has_down)
        def _():
            weight_copy(plane, half, weight_ref.at[half], 1, below).start()

    def send_first(chunk, carry):
        send_chunk(chunk)
        send_own_weights(chunk)
        return carry

    lax.fori_loop(0, halves, send_first, 0)

    own_weights = pltpu.make_async_copy(weight_ref, weights.at[plane], wlocal_sem)
    own_weights.start()

    def relay_weights(step, half):
        @pl.when(plane - step >= 0)
        def _():
            shard = weights.at[plane - step, half]
            pltpu.make_async_copy(shard, shard, wrecv_sem.at[plane - step, half]).wait()

            @pl.when(has_up)
            def _():
                weight_copy(plane - step, half, shard, 0, above).start()

        @pl.when(plane + step < planes)
        def _():
            shard = weights.at[plane + step, half]
            pltpu.make_async_copy(shard, shard, wrecv_sem.at[plane + step, half]).wait()

            @pl.when(has_down)
            def _():
                weight_copy(plane + step, half, shard, 1, below).start()

    @pl.when(jnp.logical_not(has_up))
    def _():
        queries_up[...] = jnp.zeros_like(queries_up)

    @pl.when(jnp.logical_not(has_down))
    def _():
        up_into[...] = jnp.zeros_like(up_into)
        up_stats_into[...] = jnp.zeros_like(up_stats_into)

    gets_down = jnp.logical_and(has_up, side == 1)
    gives_down = jnp.logical_and(has_down, side == 1)

    @pl.when(jnp.logical_not(gets_down))
    def _():
        down_into[...] = jnp.zeros_like(down_into)
        down_stats_into[...] = jnp.zeros_like(down_stats_into)

    slots = lengths_ref.shape[1]
    before = lax.broadcasted_iota(jnp.int32, (slots, slots), 0)
    after = lax.broadcasted_iota(jnp.int32, (slots, slots), 1)
    lengths = lengths_ref[...].astype(jnp.float32)
    all_ends = jnp.dot(
        lengths.astype(jnp.bfloat16),
        jnp.where(before <= after, 1.0, 0.0).astype(jnp.bfloat16),
        preferred_element_type=jnp.float32,
    )
    base = plane * span
    far = 4 * planes * span

    def places_of(row, shift):
        ends = all_ends[row : row + 1].astype(jnp.int32)
        starts = ends - lengths_ref[row : row + 1]
        wide_places = base + shift + lax.broadcasted_iota(jnp.int32, (span, slots), 0)
        inside = (wide_places >= starts) & (wide_places < ends)
        place = base + shift + lax.broadcasted_iota(jnp.int32, (span, 1), 0)
        first = jnp.sum(jnp.where(inside, starts, 0), axis=1, keepdims=True)
        last = jnp.sum(jnp.where(inside, ends, 0), axis=1, keepdims=True) - 1
        return first - base, place - base, first + last - place - base

    k_places = lax.broadcasted_iota(jnp.int32, (span, span), 1)
    q_places = lax.broadcasted_iota(jnp.int32, (span, span), 0)
    places = lax.broadcasted_iota(jnp.int32, (span, 2 * span), 1)
    for row in range(rows):
        first, place, mirror = places_of(row, 0)
        allowed = (k_places >= first) & (k_places <= q_places)
        own_bias[row] = jnp.where(allowed, jnp.float32(0), jnp.float32(-1e30))
        source = jnp.where(side == 0, place, mirror)
        own_moves[row] = jnp.where(places == source, 1.0, 0.0).astype(jnp.bfloat16)
        first, place, mirror = places_of(row, span)
        first = jnp.where(has_up, first, far)
        up_bias[row] = jnp.where(k_places >= first, jnp.float32(0), jnp.float32(-1e30))
        source = jnp.where(side == 0, place, mirror)
        up_moves[row] = jnp.where(places == source, 1.0, 0.0).astype(jnp.bfloat16)
        first, place, mirror = places_of(row, -span)
        source = jnp.where(gives_down, mirror, far)
        down_moves[row] = jnp.where(k_places == source, 1.0, 0.0).astype(jnp.bfloat16)

    def attend(chunk, part, q_of, bias_ref):
        def attend_row(row, inner):
            lane = lax.broadcasted_iota(jnp.int32, (span, head_width), 1) - row * 8
            stats = jnp.where(lane == 6, jnp.float32(1), jnp.float32(0))
            for head in range(2):
                lanes = slice(head * head_width, (head + 1) * head_width)
                scores = lax.dot_general(
                    q_of(row, lanes),
                    states[chunk, 1, row, :, lanes],
                    (((1,), (1,)), ((), ())),
                    preferred_element_type=jnp.float32,
                )
                scores = scores * scale + bias_ref[row]
                top = jnp.max(scores, axis=1, keepdims=True)
                raised = jnp.exp(scores - top)
                total = jnp.sum(raised, axis=1, keepdims=True)
                raw[chunk, row, part * span : (part + 1) * span, lanes] = jnp.dot(
                    (raised * (1.0 / total)).astype(jnp.bfloat16),
                    states[chunk, 2, row, :, lanes],
                    preferred_element_type=jnp.float32,
                ).astype(jnp.bfloat16)
                level = top + jnp.log(total)
                for digit in range(3):
                    rounded = level.astype(jnp.bfloat16).astype(jnp.float32)
                    stats = jnp.where(lane == head * 3 + digit, rounded, stats)
                    level = level - rounded
            raw[chunk, row, part * span : (part + 1) * span, wide:] = stats.astype(jnp.bfloat16)
            return inner

        lax.fori_loop(0, rows, attend_row, 0)

    def query_copy(chunk):
        return pltpu.make_async_remote_copy(
            src_ref=states.at[chunk, 0],
            dst_ref=queries_up.at[chunk],
            send_sem=qsend_sem.at[chunk],
            recv_sem=qrecv_sem.at[chunk],
            **below,
        )

    def context_copies(chunk, sources, targets, sends, receives, device):
        return [
            pltpu.make_async_remote_copy(
                src_ref=source.at[chunk],
                dst_ref=target.at[chunk],
                send_sem=sends.at[chunk, index],
                recv_sem=receives.at[chunk, index],
                **device,
            )
            for index, (source, target) in enumerate(zip(sources, targets))
        ]

    def up_copies(chunk):
        return context_copies(
            chunk, (up_from, up_stats_from), (up_into, up_stats_into), usend_sem, urecv_sem, above
        )

    def down_copies(chunk):
        return context_copies(
            chunk, (down_from, down_stats_from), (down_into, down_stats_into), dsend_sem, drecv_sem, below
        )

    def wait_for(refs, sems, chunk):
        for index, ref in enumerate(refs):
            pltpu.make_async_copy(ref.at[chunk], ref.at[chunk], sems.at[chunk, index]).wait()

    def exchange(chunk, head):
        column = pl.multiple_of((2 * head + side) * head_width, head_width)
        there = feats.at[chunk, :, :, pl.ds(column, head_width)]
        return pltpu.make_async_remote_copy(
            src_ref=there,
            dst_ref=there,
            send_sem=csend_sem.at[chunk, head],
            recv_sem=crecv_sem.at[chunk, head],
            **across,
        )

    def local_stage(chunk):
        others = states.at[chunk, :, :, pl.ds(0, span - piece), :]
        pltpu.make_async_copy(others, others, recv_sem.at[chunk]).wait()
        mine = states.at[chunk, :, :, pl.ds(0, piece), :]
        pltpu.make_async_copy(mine, mine, local_sem.at[chunk]).wait()

        @pl.when(has_down)
        def _():
            query_copy(chunk).start()

        @pl.when(chunk + halves < chunks)
        def _():
            send_chunk(chunk + halves)

        attend(chunk, 0, lambda row, lanes: states[chunk, 0, row, :, lanes], own_bias)

    def moved_part(moves, source, chunk, row, target):
        moved = jnp.dot(moves[row], source, preferred_element_type=jnp.float32)
        target[chunk, row] = moved[:, :wide].astype(jnp.bfloat16)
        return moved[:, wide:]

    def cross_stage(chunk):
        @pl.when(has_up)
        def _():
            pltpu.make_async_copy(
                queries_up.at[chunk], queries_up.at[chunk], qrecv_sem.at[chunk]
            ).wait()

        attend(chunk, 1, lambda row, lanes: queries_up[chunk, row, :, lanes], up_bias)

        @pl.when(has_up)
        def _():
            stats = 0.0
            for row in range(rows):
                stats = stats + moved_part(up_moves, raw[chunk, row], chunk, row, up_from)
            up_stats_from[chunk] = stats.astype(jnp.bfloat16)
            for copy in up_copies(chunk):
                copy.start()

        @pl.when(gives_down)
        def _():
            stats = 0.0
            for row in range(rows):
                stats = stats + moved_part(down_moves, raw[chunk, row, :span], chunk, row, down_from)
            down_stats_from[chunk] = stats.astype(jnp.bfloat16)
            for copy in down_copies(chunk):
                copy.start()

        stats = 0.0
        for row in range(rows):
            stats = stats + moved_part(own_moves, raw[chunk, row], chunk, row, own)
        own_stats[chunk] = stats.astype(jnp.bfloat16)

    def merge_stage(chunk):
        @pl.when(has_down)
        def _():
            wait_for((up_into, up_stats_into), urecv_sem, chunk)

        @pl.when(gets_down)
        def _():
            wait_for((down_into, down_stats_into), drecv_sem, chunk)

        for row in range(rows):
            parts = (own, up_into, down_into)
            stats = [
                ref[chunk].astype(jnp.float32)[:, row * 8 : row * 8 + 8]
                for ref in (own_stats, up_stats_into, down_stats_into)
            ]
            for head in range(2):
                lanes = slice(head * head_width, (head + 1) * head_width)
                levels = []
                for stat in stats:
                    level = stat[:, head * 3 : head * 3 + 1] + stat[:, head * 3 + 1 : head * 3 + 2]
                    level = level + stat[:, head * 3 + 2 : head * 3 + 3]
                    levels.append(jnp.where(stat[:, 6:7] > 0.5, level, jnp.float32(-3e30)))
                top = jnp.maximum(jnp.maximum(levels[0], levels[1]), levels[2])
                shares = [jnp.exp(level - top) for level in levels]
                norm = 1.0 / (shares[0] + shares[1] + shares[2])
                value = 0.0
                for part, share in zip(parts, shares):
                    value = value + part[chunk, row, :, lanes].astype(jnp.float32) * (share * norm)
                value = value.astype(jnp.bfloat16)
                column = pl.multiple_of((2 * head + side) * head_width, head_width)
                for owner in range(members):
                    feats[chunk, owner, row * piece : (row + 1) * piece, pl.ds(column, head_width)] = value[
                        owner * piece : (owner + 1) * piece
                    ]
        for head in range(2):
            exchange(chunk, head).start()

    def stage(step, carry):
        @pl.when(step < chunks)
        def _():
            local_stage(step)

        for late in range(1, planes - 1):

            @pl.when(step == late)
            def _():
                for half in range(halves):
                    relay_weights(late, half)

        @pl.when(jnp.logical_and(step >= 1, step <= chunks))
        def _():
            cross_stage(step - 1)

        @pl.when(step >= 2)
        def _():
            merge_stage(step - 2)

        return carry

    lax.fori_loop(0, chunks + 2, stage, 0)

    own_weights.wait()

    def arrive(chunk, carry):
        for head in range(2):
            column = pl.multiple_of((2 * head + 1 - side) * head_width, head_width)
            there = feats.at[chunk, :, :, pl.ds(column, head_width)]
            pltpu.make_async_copy(there, there, crecv_sem.at[chunk, head]).wait()
        return carry

    lax.fori_loop(0, chunks, arrive, 0)

    low_half = plane < planes // 2
    last = jnp.where(low_half, chunks - 1, 0)

    def join_early(owner, carry):
        for half in range(halves):
            total = 0.0
            for step in range(chunks - 1):
                chunk = jnp.where(low_half, step, chunks - 1 - step)
                total = total + jnp.dot(
                    feats[chunk, owner], weights[chunk, half], preferred_element_type=jnp.float32
                )
            sums[half, owner] = total
        return carry

    lax.fori_loop(0, members, join_early, 0)

    def partial_copy(half, owner):
        return pltpu.make_async_remote_copy(
            src_ref=partials.at[half, owner],
            dst_ref=arrived.at[half, member],
            send_sem=psend_sem.at[half],
            recv_sem=precv_sem.at[half],
            **at(plane * members + owner),
        )

    def join_half(half, carry):
        relay_weights(planes - 1, half)

        def join_last(step, inner):
            owner = lax.rem(member + 1 + step, members)
            total = sums[half, owner] + jnp.dot(
                feats[last, owner], weights[last, half], preferred_element_type=jnp.float32
            )
            partials[half, owner] = total.astype(jnp.bfloat16)

            @pl.when(step < members - 1)
            def _():
                partial_copy(half, owner).start()

            return inner

        lax.fori_loop(0, members, join_last, 0)
        arrived[half, member] = partials[half, member]
        return carry

    lax.fori_loop(0, halves, join_half, 0)
    columns = out_ref.shape[2] // halves
    for half in range(halves):
        incoming = arrived.at[half, pl.ds(0, members - 1)]
        pltpu.make_async_copy(incoming, incoming, precv_sem.at[half]).wait()
        for row in range(rows):
            total = 0.0
            for source in range(members):
                total = total + arrived[half, source, row * piece : (row + 1) * piece, :].astype(
                    jnp.float32
                )
            gate, up = total[:, :columns], total[:, columns:]
            out_ref[row, :, half * columns : (half + 1) * columns] = (
                gate / (1.0 + jnp.exp(-gate)) * up
            ).astype(jnp.bfloat16)

    def finish(chunk, carry):
        others = states.at[chunk, :, :, pl.ds(0, span - piece), :]
        pltpu.make_async_copy(others, others, send_sem.at[chunk]).wait()
        for head in range(2):
            exchange(chunk, head).wait_send()

        @pl.when(has_up)
        def _():
            for copy in up_copies(chunk):
                copy.wait_send()

        @pl.when(has_down)
        def _():
            query_copy(chunk).wait_send()

        @pl.when(gives_down)
        def _():
            for copy in down_copies(chunk):
                copy.wait_send()

        return carry

    lax.fori_loop(0, chunks, finish, 0)
    for step in range(planes):

        @pl.when(jnp.logical_and(has_up, plane - step >= 0))
        def _():
            for half in range(halves):
                weight_copy(plane - step, half, weights.at[plane - step, half], 0, above).wait_send()

        @pl.when(jnp.logical_and(has_down, plane + step < planes))
        def _():
            for half in range(halves):
                weight_copy(plane + step, half, weights.at[plane + step, half], 1, below).wait_send()

    for half in range(halves):
        incoming = arrived.at[half, pl.ds(0, members - 1)]
        pltpu.make_async_copy(incoming, incoming, psend_sem.at[half]).wait()


def fused_body(queries, key_states, value_vectors, hypothesis_lengths, join_weight):
    rows, piece, width = (queries.shape[1], queries.shape[2], queries.shape[3])
    devices = lax.axis_size("seq")
    planes, members = devices // PACKED_ROWS, PACKED_ROWS
    head_width = width // ATTENTION_HEADS
    wide = 2 * head_width
    chunks = width // (members * wide)
    span = members * piece
    halves = 2
    weight_rows, _, columns = join_weight.shape
    part = columns // halves
    by_halves = jnp.transpose(join_weight.reshape(weight_rows, 2, halves, part), (2, 0, 1, 3))
    geometry = (planes, rows, members, piece, head_width, chunks, halves)

    def vmem(*shape):
        return pltpu.VMEM(shape, jnp.bfloat16)

    dma = pltpu.SemaphoreType.DMA
    context = (chunks, rows, span, wide)
    stats = (chunks, span, head_width)
    return pl.pallas_call(
        functools.partial(pair_kernel, geometry),
        out_shape=jax.ShapeDtypeStruct((rows, piece, columns), jnp.bfloat16),
        in_specs=[pl.BlockSpec(memory_space=pltpu.VMEM)] + [pl.BlockSpec(memory_space=pl.ANY)] * 4,
        out_specs=pl.BlockSpec(memory_space=pltpu.VMEM),
        scratch_shapes=[
            vmem(chunks, 3, rows, span, wide),
            vmem(*context),
            vmem(chunks, rows, 2 * span, wide + head_width),
            *[vmem(*context)] * 5,
            *[vmem(*stats)] * 5,
            vmem(planes, halves, weight_rows, 2 * part),
            vmem(chunks, members, rows * piece, 2 * wide),
            pltpu.VMEM((halves, members, rows * piece, 2 * part), jnp.float32),
            vmem(halves, members, rows * piece, 2 * part),
            vmem(halves, members, rows * piece, 2 * part),
            vmem(rows, span, 2 * span),
            vmem(rows, span, 2 * span),
            vmem(rows, span, span),
            pltpu.VMEM((rows, span, span), jnp.float32),
            pltpu.VMEM((rows, span, span), jnp.float32),
            dma((chunks,)),
            dma((chunks,)),
            dma((chunks,)),
            dma((chunks,)),
            dma((chunks,)),
            dma((chunks, 2)),
            dma((chunks, 2)),
            dma((chunks, 2)),
            dma((chunks, 2)),
            dma((2, planes, halves)),
            dma((planes, halves)),
            dma,
            dma((chunks, 2)),
            dma((chunks, 2)),
            dma((halves,)),
            dma((halves,)),
        ],
        compiler_params=pltpu.CompilerParams(
            collective_id=0, has_side_effects=True, vmem_limit_bytes=60 * 1024 * 1024
        ),
    )(
        hypothesis_lengths,
        queries,
        key_states,
        value_vectors,
        by_halves.reshape(halves, weight_rows, 2 * part),
    )


def fits_kernel(mesh):
    planes = mesh.shape["seq"] // PACKED_ROWS
    return ATTENTION_HEADS // planes == 2 * PACKED_ROWS


def solution(mesh):
    return jax.shard_map(
        fused_body if fits_kernel(mesh) else body,
        mesh=mesh,
        in_specs=(
            P("dir", None, "seq", None),
            P("dir", None, "seq", None),
            P("dir", None, "seq", None),
            P(),
            P("seq", None, "dir"),
        ),
        out_specs=P(None, "seq", "dir"),
        check_vma=False,
    )
```

```python
import functools
import math

import jax
import jax.numpy as jnp
from jax import lax
from jax.experimental import pallas as pl
from jax.experimental.pallas import tpu as pltpu
from jax.sharding import PartitionSpec as P

ATTENTION_HEADS = 32
LONGEST_TOKENS = 256
PACKED_ROWS = 4


def swapped(array, axis, stride):
    return lax.ppermute(array, axis, [(i, i ^ 1 << stride) for i in range(lax.axis_size(axis))])


def hypothesis_tables(length_list, row_len):
    ends = jnp.cumsum(length_list)
    starts = ends - length_list
    places = jnp.arange(row_len, dtype=jnp.int32)
    inside = (places[:, None] >= starts[None, :]) & (places[:, None] < ends[None, :])
    first = jnp.sum(jnp.where(inside, starts[None, :], 0), axis=1)
    after = jnp.sum(jnp.where(inside, ends[None, :], 0), axis=1)
    mirror = first + after - 1 - places
    return (first, mirror)


def attend_group(query_row, k_row, v_row, first):
    row_len = query_row.shape[0]
    block_item = min(512, row_len)
    token_span = min(block_item + LONGEST_TOKENS, row_len)
    scale = 1.0 / math.sqrt(query_row.shape[2])

    def single_block(index):
        q_start = index * block_item
        k_start = jnp.maximum(q_start + block_item - token_span, 0)
        q_part = lax.dynamic_slice_in_dim(query_row, q_start, block_item, 0)
        k_part = lax.dynamic_slice_in_dim(k_row, k_start, token_span, 0)
        v_part = lax.dynamic_slice_in_dim(v_row, k_start, token_span, 0)
        scores = (
            jnp.einsum("qhc,khc->hqk", q_part, k_part, preferred_element_type=jnp.float32) * scale
        )
        q_places = q_start + jnp.arange(block_item, dtype=jnp.int32)
        k_places = k_start + jnp.arange(token_span, dtype=jnp.int32)
        starts = lax.dynamic_slice_in_dim(first, q_start, block_item, 0)
        allowed = (k_places[None, :] >= starts[:, None]) & (k_places[None, :] <= q_places[:, None])
        scores = jnp.where(allowed[None], scores, jnp.float32(-1e30))
        top = jnp.max(scores, axis=2, keepdims=True)
        raised = jnp.exp(scores - top)
        weights = (raised / jnp.sum(raised, axis=2, keepdims=True)).astype(jnp.bfloat16)
        return jnp.einsum(
            "hqk,khc->qhc", weights, v_part, preferred_element_type=jnp.float32
        ).astype(jnp.bfloat16)

    block_list = lax.map(single_block, jnp.arange(row_len // block_item, dtype=jnp.int32))
    return block_list.reshape(row_len, query_row.shape[1], query_row.shape[2])


def body(queries, key_states, value_vectors, hypothesis_lengths, join_weight):
    rows, piece, width = (queries.shape[1], queries.shape[2], queries.shape[3])
    devices = lax.axis_size("seq")
    groups = devices // rows
    head_width = width // ATTENTION_HEADS
    pair = width // groups
    heads_here = pair // head_width
    row_bits = rows.bit_length() - 1
    place = lax.axis_index("seq")
    row = place % rows
    row_len = devices * piece

    def regroup(states):
        states = states.reshape(rows, piece, groups, pair)
        return jnp.transpose(states, (2, 0, 1, 3)).reshape(groups * rows, piece, pair)

    q_all, k_all, v_all = (
        lax.all_to_all(regroup(queries[0]), "seq", split_axis=0, concat_axis=1, tiled=True),
        lax.all_to_all(regroup(key_states[0]), "seq", split_axis=0, concat_axis=1, tiled=True),
        lax.all_to_all(regroup(value_vectors[0]), "seq", split_axis=0, concat_axis=1, tiled=True),
    )
    block_rows = join_weight
    for bit in range(row_bits):
        partner = swapped(block_rows, "seq", bit)
        lower = place // 2**bit % 2 == 0
        block_rows = jnp.where(
            lower,
            jnp.concatenate([block_rows, partner], 0),
            jnp.concatenate([partner, block_rows], 0),
        )
    length_list = lax.dynamic_index_in_dim(hypothesis_lengths, row, 0, keepdims=False)
    first, mirror = hypothesis_tables(length_list, row_len)
    array_shape = (row_len, heads_here, head_width)
    context_vectors = attend_group(
        q_all.reshape(array_shape), k_all.reshape(array_shape), v_all.reshape(array_shape), first
    )
    other = swapped(context_vectors, "dir", 0)
    side = lax.axis_index("dir")
    left_side = jnp.where(side == 0, context_vectors, other)
    right_side = jnp.where(side == 0, other, context_vectors)
    right_side = jnp.take(right_side, mirror, axis=0)
    feature_rows = jnp.stack([left_side, right_side], axis=2).reshape(row_len, 2 * pair)
    columns = block_rows.shape[2]
    partial_value = jnp.dot(
        feature_rows, block_rows.reshape(2 * pair, 2 * columns), preferred_element_type=jnp.float32
    ).astype(jnp.bfloat16)
    arrived = lax.all_to_all(
        partial_value.reshape(devices, piece, 2 * columns),
        "seq",
        split_axis=0,
        concat_axis=0,
        tiled=True,
    )
    totals = jnp.sum(arrived.reshape(groups, rows, piece, 2 * columns).astype(jnp.float32), axis=0)
    joined = jax.nn.silu(totals[..., :columns]) * totals[..., columns:]
    return joined.astype(jnp.bfloat16)


def pair_kernel(
    geometry, lengths_ref, q_ref, k_ref, v_ref, weight_ref, out_ref,
    states, queries_up, raw, own, up_from, up_into, down_from, down_into,
    own_stats, up_stats_from, up_stats_into, down_stats_from, down_stats_into,
    weights, feats, sums, partials, arrived, own_moves, up_moves, down_moves, own_bias, up_bias,
    send_sem, recv_sem, local_sem, qsend_sem, qrecv_sem, usend_sem, urecv_sem, dsend_sem, drecv_sem,
    wsend_sem, wrecv_sem, wlocal_sem, csend_sem, crecv_sem, psend_sem, precv_sem,
):
    planes, rows, members, piece, head_width, chunks, halves = geometry
    side = lax.axis_index("dir")
    me = lax.axis_index("seq")
    plane, member = lax.div(me, members), lax.rem(me, members)
    wide = 2 * head_width
    span = members * piece
    scale = 1.0 / math.sqrt(head_width)
    has_up, has_down = plane < planes - 1, plane > 0

    def at(peer):
        return {"device_id": (side, peer), "device_id_type": pl.DeviceIdType.MESH}

    def beside(step):
        return at(plane * members + lax.rem(member + step, members))

    above, below = at(me + members), at(me - members)
    across = {"device_id": (1 - side, me), "device_id_type": pl.DeviceIdType.MESH}

    barrier = pltpu.get_barrier_semaphore()
    for step in range(1, members):
        pl.semaphore_signal(barrier, inc=1, **beside(step))
    pl.semaphore_signal(barrier, inc=1, **across)

    @pl.when(has_up)
    def _():
        pl.semaphore_signal(barrier, inc=1, **above)

    @pl.when(has_down)
    def _():
        pl.semaphore_signal(barrier, inc=1, **below)

    pl.semaphore_wait(barrier, members + jnp.where(has_up, 1, 0) + jnp.where(has_down, 1, 0))

    def weight_copy(shard, half, source, way, target):
        return pltpu.make_async_remote_copy(
            src_ref=source,
            dst_ref=weights.at[shard, half],
            send_sem=wsend_sem.at[way, shard, half],
            recv_sem=wrecv_sem.at[shard, half],
            **target,
        )

    def input_column(chunk, owner):
        return pl.ds(pl.multiple_of((chunk * members + owner) * wide, wide), wide)

    def landing(chunk, index):
        return states.at[chunk, index, :, pl.ds(pl.multiple_of(member * piece, piece), piece), :]

    def send_chunk(chunk):
        for step in range(1, members):
            owner = lax.rem(member + step, members)
            for index, ref in enumerate((q_ref, k_ref, v_ref)):
                pltpu.make_async_remote_copy(
                    src_ref=ref.at[0, :, :, input_column(chunk, owner)],
                    dst_ref=landing(chunk, index),
                    send_sem=send_sem.at[chunk],
                    recv_sem=recv_sem.at[chunk],
                    **beside(step),
                ).start()
        for index, ref in enumerate((q_ref, k_ref, v_ref)):
            pltpu.make_async_copy(
                ref.at[0, :, :, input_column(chunk, member)], landing(chunk, index), local_sem.at[chunk]
            ).start()

    def send_own_weights(half):
        @pl.when(has_up)
        def _():
            weight_copy(plane, half, weight_ref.at[half], 0, above).start()

        @pl.when(has_down)
        def _():
            weight_copy(plane, half, weight_ref.at[half], 1, below).start()

    def send_first(chunk, carry):
        send_chunk(chunk)
        send_own_weights(chunk)
        return carry

    lax.fori_loop(0, halves, send_first, 0)

    own_weights = pltpu.make_async_copy(weight_ref, weights.at[plane], wlocal_sem)
    own_weights.start()

    def relay_weights(step, half):
        @pl.when(plane - step >= 0)
        def _():
            shard = weights.at[plane - step, half]
            pltpu.make_async_copy(shard, shard, wrecv_sem.at[plane - step, half]).wait()

            @pl.when(has_up)
            def _():
                weight_copy(plane - step, half, shard, 0, above).start()

        @pl.when(plane + step < planes)
        def _():
            shard = weights.at[plane + step, half]
            pltpu.make_async_copy(shard, shard, wrecv_sem.at[plane + step, half]).wait()

            @pl.when(has_down)
            def _():
                weight_copy(plane + step, half, shard, 1, below).start()

    @pl.when(jnp.logical_not(has_up))
    def _():
        queries_up[...] = jnp.zeros_like(queries_up)

    @pl.when(jnp.logical_not(has_down))
    def _():
        up_into[...] = jnp.zeros_like(up_into)
        up_stats_into[...] = jnp.zeros_like(up_stats_into)

    gets_down = jnp.logical_and(has_up, side == 1)
    gives_down = jnp.logical_and(has_down, side == 1)

    @pl.when(jnp.logical_not(gets_down))
    def _():
        down_into[...] = jnp.zeros_like(down_into)
        down_stats_into[...] = jnp.zeros_like(down_stats_into)

    slots = lengths_ref.shape[1]
    before = lax.broadcasted_iota(jnp.int32, (slots, slots), 0)
    after = lax.broadcasted_iota(jnp.int32, (slots, slots), 1)
    lengths = lengths_ref[...].astype(jnp.float32)
    all_ends = jnp.dot(
        lengths.astype(jnp.bfloat16),
        jnp.where(before <= after, 1.0, 0.0).astype(jnp.bfloat16),
        preferred_element_type=jnp.float32,
    )
    base = plane * span
    far = 4 * planes * span

    def places_of(row, shift):
        ends = all_ends[row : row + 1].astype(jnp.int32)
        starts = ends - lengths_ref[row : row + 1]
        wide_places = base + shift + lax.broadcasted_iota(jnp.int32, (span, slots), 0)
        inside = (wide_places >= starts) & (wide_places < ends)
        place = base + shift + lax.broadcasted_iota(jnp.int32, (span, 1), 0)
        first = jnp.sum(jnp.where(inside, starts, 0), axis=1, keepdims=True)
        last = jnp.sum(jnp.where(inside, ends, 0), axis=1, keepdims=True) - 1
        return first - base, place - base, first + last - place - base

    k_places = lax.broadcasted_iota(jnp.int32, (span, span), 1)
    q_places = lax.broadcasted_iota(jnp.int32, (span, span), 0)
    places = lax.broadcasted_iota(jnp.int32, (span, 2 * span), 1)
    for row in range(rows):
        first, place, mirror = places_of(row, 0)
        allowed = (k_places >= first) & (k_places <= q_places)
        own_bias[row] = jnp.where(allowed, jnp.float32(0), jnp.float32(-1e30))
        source = jnp.where(side == 0, place, mirror)
        own_moves[row] = jnp.where(places == source, 1.0, 0.0).astype(jnp.bfloat16)
        first, place, mirror = places_of(row, span)
        first = jnp.where(has_up, first, far)
        up_bias[row] = jnp.where(k_places >= first, jnp.float32(0), jnp.float32(-1e30))
        source = jnp.where(side == 0, place, mirror)
        up_moves[row] = jnp.where(places == source, 1.0, 0.0).astype(jnp.bfloat16)
        first, place, mirror = places_of(row, -span)
        source = jnp.where(gives_down, mirror, far)
        down_moves[row] = jnp.where(k_places == source, 1.0, 0.0).astype(jnp.bfloat16)

    def attend(chunk, part, q_of, bias_ref):
        reach = span // 2

        def attend_row(row, inner):
            lane = lax.broadcasted_iota(jnp.int32, (reach, head_width), 1) - row * 8
            mine = (lane >= 0) & (lane < 6)
            for half in range(2):
                at_rows = slice(half * reach, (half + 1) * reach)
                keys = slice(0, (half + 1) * reach) if part == 0 else slice(half * reach, span)
                placed = slice(part * span + half * reach, part * span + (half + 1) * reach)
                tops, totals = [], []
                for head in range(2):
                    lanes = slice(head * head_width, (head + 1) * head_width)
                    scores = lax.dot_general(
                        q_of(row, at_rows, lanes),
                        states[chunk, 1, row, keys, lanes],
                        (((1,), (1,)), ((), ())),
                        preferred_element_type=jnp.float32,
                    )
                    scores = scores * scale + bias_ref[row, at_rows, keys]
                    top = jnp.max(scores, axis=1, keepdims=True)
                    raised = jnp.exp(scores - top)
                    total = jnp.sum(raised, axis=1, keepdims=True)
                    raw[chunk, row, placed, lanes] = jnp.dot(
                        (raised * (1.0 / total)).astype(jnp.bfloat16),
                        states[chunk, 2, row, keys, lanes],
                        preferred_element_type=jnp.float32,
                    ).astype(jnp.bfloat16)
                    tops.append(top)
                    totals.append(total)
                level = jnp.where(lane >= 3, tops[1], tops[0]) + jnp.log(
                    jnp.where(lane >= 3, totals[1], totals[0])
                )
                high = level.astype(jnp.bfloat16).astype(jnp.float32)
                level = level - high
                middle = level.astype(jnp.bfloat16).astype(jnp.float32)
                low = level - middle
                digits = jnp.where(
                    (lane == 0) | (lane == 3), high, jnp.where((lane == 1) | (lane == 4), middle, low)
                )
                digits = jnp.where(mine, digits, jnp.where(lane == 6, 1.0, 0.0))
                raw[chunk, row, placed, wide:] = digits.astype(jnp.bfloat16)
            return inner

        lax.fori_loop(0, rows, attend_row, 0)

    def query_copy(chunk):
        return pltpu.make_async_remote_copy(
            src_ref=states.at[chunk, 0],
            dst_ref=queries_up.at[chunk],
            send_sem=qsend_sem.at[chunk],
            recv_sem=qrecv_sem.at[chunk],
            **below,
        )

    def context_copies(chunk, sources, targets, sends, receives, device):
        return [
            pltpu.make_async_remote_copy(
                src_ref=source.at[chunk],
                dst_ref=target.at[chunk],
                send_sem=sends.at[chunk, index],
                recv_sem=receives.at[chunk, index],
                **device,
            )
            for index, (source, target) in enumerate(zip(sources, targets))
        ]

    def up_copies(chunk):
        return context_copies(
            chunk, (up_from, up_stats_from), (up_into, up_stats_into), usend_sem, urecv_sem, above
        )

    def down_copies(chunk):
        return context_copies(
            chunk, (down_from, down_stats_from), (down_into, down_stats_into), dsend_sem, drecv_sem, below
        )

    def wait_for(refs, sems, chunk):
        for index, ref in enumerate(refs):
            pltpu.make_async_copy(ref.at[chunk], ref.at[chunk], sems.at[chunk, index]).wait()

    def exchange(chunk, head):
        column = pl.multiple_of((2 * head + side) * head_width, head_width)
        there = feats.at[chunk, :, :, pl.ds(column, head_width)]
        return pltpu.make_async_remote_copy(
            src_ref=there,
            dst_ref=there,
            send_sem=csend_sem.at[chunk, head],
            recv_sem=crecv_sem.at[chunk, head],
            **across,
        )

    def local_stage(chunk):
        others = states.at[chunk, :, :, pl.ds(0, span - piece), :]
        pltpu.make_async_copy(others, others, recv_sem.at[chunk]).wait()
        mine = states.at[chunk, :, :, pl.ds(0, piece), :]
        pltpu.make_async_copy(mine, mine, local_sem.at[chunk]).wait()

        @pl.when(has_down)
        def _():
            query_copy(chunk).start()

        @pl.when(chunk + halves < chunks)
        def _():
            send_chunk(chunk + halves)

        attend(chunk, 0, lambda row, at_rows, lanes: states[chunk, 0, row, at_rows, lanes], own_bias)

    def moved_part(moves, source, chunk, row, target):
        moved = jnp.dot(moves[row], source, preferred_element_type=jnp.float32)
        target[chunk, row] = moved[:, :wide].astype(jnp.bfloat16)
        return moved[:, wide:]

    def cross_stage(chunk):
        @pl.when(has_up)
        def _():
            pltpu.make_async_copy(
                queries_up.at[chunk], queries_up.at[chunk], qrecv_sem.at[chunk]
            ).wait()

        attend(chunk, 1, lambda row, at_rows, lanes: queries_up[chunk, row, at_rows, lanes], up_bias)

        @pl.when(has_up)
        def _():
            stats = 0.0
            for row in range(rows):
                stats = stats + moved_part(up_moves, raw[chunk, row], chunk, row, up_from)
            up_stats_from[chunk] = stats.astype(jnp.bfloat16)
            for copy in up_copies(chunk):
                copy.start()

        @pl.when(gives_down)
        def _():
            stats = 0.0
            for row in range(rows):
                stats = stats + moved_part(down_moves, raw[chunk, row, :span], chunk, row, down_from)
            down_stats_from[chunk] = stats.astype(jnp.bfloat16)
            for copy in down_copies(chunk):
                copy.start()

        stats = 0.0
        for row in range(rows):
            stats = stats + moved_part(own_moves, raw[chunk, row], chunk, row, own)
        own_stats[chunk] = stats.astype(jnp.bfloat16)

    def merge_stage(chunk):
        @pl.when(has_down)
        def _():
            wait_for((up_into, up_stats_into), urecv_sem, chunk)

        @pl.when(gets_down)
        def _():
            wait_for((down_into, down_stats_into), drecv_sem, chunk)

        lane_in = lax.broadcasted_iota(jnp.int32, (head_width, head_width), 0)
        lane_out = lax.broadcasted_iota(jnp.int32, (head_width, head_width), 1)
        same_row = lane_in // 8 == lane_out // 8
        digit_in, digit_out = lane_in % 8, lane_out % 8
        same_head = (digit_in < 6) & ((digit_in >= 3) == (digit_out >= 3))
        gather = jnp.where(same_row & same_head, 1.0, 0.0).astype(jnp.bfloat16)
        marks = jnp.where(same_row & (digit_in == 6), 1.0, 0.0).astype(jnp.bfloat16)
        levels = []
        for ref in (own_stats, up_stats_into, down_stats_into):
            stat = ref[chunk]
            level = jnp.dot(stat, gather, preferred_element_type=jnp.float32)
            present = jnp.dot(stat, marks, preferred_element_type=jnp.float32)
            levels.append(jnp.where(present > 0.5, level, jnp.float32(-3e30)))
        top = jnp.maximum(jnp.maximum(levels[0], levels[1]), levels[2])
        shares = [jnp.exp(level - top) for level in levels]
        norm = 1.0 / (shares[0] + shares[1] + shares[2])
        shares = [share * norm for share in shares]
        for row in range(rows):
            for head in range(2):
                lanes = slice(head * head_width, (head + 1) * head_width)
                lane = row * 8 + head * 3
                value = 0.0
                for part, share in zip((own, up_into, down_into), shares):
                    value = value + part[chunk, row, :, lanes].astype(jnp.float32) * share[:, lane : lane + 1]
                value = value.astype(jnp.bfloat16)
                column = pl.multiple_of((2 * head + side) * head_width, head_width)
                for owner in range(members):
                    feats[chunk, owner, row * piece : (row + 1) * piece, pl.ds(column, head_width)] = value[
                        owner * piece : (owner + 1) * piece
                    ]
        for head in range(2):
            exchange(chunk, head).start()

    def stage(step, carry):
        @pl.when(step < chunks)
        def _():
            local_stage(step)

        for late in range(1, planes - 1):

            @pl.when(step == late)
            def _():
                for half in range(halves):
                    relay_weights(late, half)

        @pl.when(jnp.logical_and(step >= 1, step <= chunks))
        def _():
            cross_stage(step - 1)

        @pl.when(step >= 2)
        def _():
            merge_stage(step - 2)

        return carry

    lax.fori_loop(0, chunks + 2, stage, 0)

    own_weights.wait()

    def arrive(chunk, carry):
        for head in range(2):
            column = pl.multiple_of((2 * head + 1 - side) * head_width, head_width)
            there = feats.at[chunk, :, :, pl.ds(column, head_width)]
            pltpu.make_async_copy(there, there, crecv_sem.at[chunk, head]).wait()
        return carry

    lax.fori_loop(0, chunks, arrive, 0)

    low_half = plane < planes // 2
    last = jnp.where(low_half, chunks - 1, 0)

    def join_early(owner, carry):
        for half in range(halves):
            total = 0.0
            for step in range(chunks - 1):
                chunk = jnp.where(low_half, step, chunks - 1 - step)
                total = total + jnp.dot(
                    feats[chunk, owner], weights[chunk, half], preferred_element_type=jnp.float32
                )
            sums[half, owner] = total
        return carry

    lax.fori_loop(0, members, join_early, 0)

    def partial_copy(half, owner):
        return pltpu.make_async_remote_copy(
            src_ref=partials.at[half, owner],
            dst_ref=arrived.at[half, member],
            send_sem=psend_sem.at[half],
            recv_sem=precv_sem.at[half],
            **at(plane * members + owner),
        )

    def join_half(half, carry):
        relay_weights(planes - 1, half)

        def join_last(step, inner):
            owner = lax.rem(member + 1 + step, members)
            total = sums[half, owner] + jnp.dot(
                feats[last, owner], weights[last, half], preferred_element_type=jnp.float32
            )
            partials[half, owner] = total.astype(jnp.bfloat16)

            @pl.when(step < members - 1)
            def _():
                partial_copy(half, owner).start()

            return inner

        lax.fori_loop(0, members, join_last, 0)
        arrived[half, member] = partials[half, member]
        return carry

    lax.fori_loop(0, halves, join_half, 0)
    columns = out_ref.shape[2] // halves
    for half in range(halves):
        incoming = arrived.at[half, pl.ds(0, members - 1)]
        pltpu.make_async_copy(incoming, incoming, precv_sem.at[half]).wait()
        for row in range(rows):
            total = 0.0
            for source in range(members):
                total = total + arrived[half, source, row * piece : (row + 1) * piece, :].astype(
                    jnp.float32
                )
            gate, up = total[:, :columns], total[:, columns:]
            out_ref[row, :, half * columns : (half + 1) * columns] = (
                gate / (1.0 + jnp.exp(-gate)) * up
            ).astype(jnp.bfloat16)

    def finish(chunk, carry):
        others = states.at[chunk, :, :, pl.ds(0, span - piece), :]
        pltpu.make_async_copy(others, others, send_sem.at[chunk]).wait()
        for head in range(2):
            exchange(chunk, head).wait_send()

        @pl.when(has_up)
        def _():
            for copy in up_copies(chunk):
                copy.wait_send()

        @pl.when(has_down)
        def _():
            query_copy(chunk).wait_send()

        @pl.when(gives_down)
        def _():
            for copy in down_copies(chunk):
                copy.wait_send()

        return carry

    lax.fori_loop(0, chunks, finish, 0)
    for step in range(planes):

        @pl.when(jnp.logical_and(has_up, plane - step >= 0))
        def _():
            for half in range(halves):
                weight_copy(plane - step, half, weights.at[plane - step, half], 0, above).wait_send()

        @pl.when(jnp.logical_and(has_down, plane + step < planes))
        def _():
            for half in range(halves):
                weight_copy(plane + step, half, weights.at[plane + step, half], 1, below).wait_send()

    for half in range(halves):
        incoming = arrived.at[half, pl.ds(0, members - 1)]
        pltpu.make_async_copy(incoming, incoming, psend_sem.at[half]).wait()


def fused_body(queries, key_states, value_vectors, hypothesis_lengths, join_weight):
    rows, piece, width = (queries.shape[1], queries.shape[2], queries.shape[3])
    devices = lax.axis_size("seq")
    planes, members = devices // PACKED_ROWS, PACKED_ROWS
    head_width = width // ATTENTION_HEADS
    wide = 2 * head_width
    chunks = width // (members * wide)
    span = members * piece
    halves = 2
    weight_rows, _, columns = join_weight.shape
    part = columns // halves
    by_halves = jnp.transpose(join_weight.reshape(weight_rows, 2, halves, part), (2, 0, 1, 3))
    geometry = (planes, rows, members, piece, head_width, chunks, halves)

    def vmem(*shape):
        return pltpu.VMEM(shape, jnp.bfloat16)

    dma = pltpu.SemaphoreType.DMA
    context = (chunks, rows, span, wide)
    stats = (chunks, span, head_width)
    return pl.pallas_call(
        functools.partial(pair_kernel, geometry),
        out_shape=jax.ShapeDtypeStruct((rows, piece, columns), jnp.bfloat16),
        in_specs=[pl.BlockSpec(memory_space=pltpu.VMEM)] + [pl.BlockSpec(memory_space=pl.ANY)] * 4,
        out_specs=pl.BlockSpec(memory_space=pltpu.VMEM),
        scratch_shapes=[
            vmem(chunks, 3, rows, span, wide),
            vmem(*context),
            vmem(chunks, rows, 2 * span, wide + head_width),
            *[vmem(*context)] * 5,
            *[vmem(*stats)] * 5,
            vmem(planes, halves, weight_rows, 2 * part),
            vmem(chunks, members, rows * piece, 2 * wide),
            pltpu.VMEM((halves, members, rows * piece, 2 * part), jnp.float32),
            vmem(halves, members, rows * piece, 2 * part),
            vmem(halves, members, rows * piece, 2 * part),
            vmem(rows, span, 2 * span),
            vmem(rows, span, 2 * span),
            vmem(rows, span, span),
            pltpu.VMEM((rows, span, span), jnp.float32),
            pltpu.VMEM((rows, span, span), jnp.float32),
            dma((chunks,)),
            dma((chunks,)),
            dma((chunks,)),
            dma((chunks,)),
            dma((chunks,)),
            dma((chunks, 2)),
            dma((chunks, 2)),
            dma((chunks, 2)),
            dma((chunks, 2)),
            dma((2, planes, halves)),
            dma((planes, halves)),
            dma,
            dma((chunks, 2)),
            dma((chunks, 2)),
            dma((halves,)),
            dma((halves,)),
        ],
        compiler_params=pltpu.CompilerParams(
            collective_id=0, has_side_effects=True, vmem_limit_bytes=60 * 1024 * 1024
        ),
    )(
        hypothesis_lengths,
        queries,
        key_states,
        value_vectors,
        by_halves.reshape(halves, weight_rows, 2 * part),
    )


def fits_kernel(mesh):
    planes = mesh.shape["seq"] // PACKED_ROWS
    return ATTENTION_HEADS // planes == 2 * PACKED_ROWS


def solution(mesh):
    return jax.shard_map(
        fused_body if fits_kernel(mesh) else body,
        mesh=mesh,
        in_specs=(
            P("dir", None, "seq", None),
            P("dir", None, "seq", None),
            P("dir", None, "seq", None),
            P(),
            P("seq", None, "dir"),
        ),
        out_specs=P(None, "seq", "dir"),
        check_vma=False,
    )
```

```python
import functools
import math

import jax
import jax.numpy as jnp
from jax import lax
from jax.experimental import pallas as pl
from jax.experimental.pallas import tpu as pltpu
from jax.sharding import PartitionSpec as P

ATTENTION_HEADS = 32
LONGEST_TOKENS = 256
PACKED_ROWS = 4


def swapped(array, axis, stride):
    return lax.ppermute(array, axis, [(i, i ^ 1 << stride) for i in range(lax.axis_size(axis))])


def hypothesis_tables(length_list, row_len):
    ends = jnp.cumsum(length_list)
    starts = ends - length_list
    places = jnp.arange(row_len, dtype=jnp.int32)
    inside = (places[:, None] >= starts[None, :]) & (places[:, None] < ends[None, :])
    first = jnp.sum(jnp.where(inside, starts[None, :], 0), axis=1)
    after = jnp.sum(jnp.where(inside, ends[None, :], 0), axis=1)
    mirror = first + after - 1 - places
    return (first, mirror)


def attend_group(query_row, k_row, v_row, first):
    row_len = query_row.shape[0]
    block_item = min(512, row_len)
    token_span = min(block_item + LONGEST_TOKENS, row_len)
    scale = 1.0 / math.sqrt(query_row.shape[2])

    def single_block(index):
        q_start = index * block_item
        k_start = jnp.maximum(q_start + block_item - token_span, 0)
        q_part = lax.dynamic_slice_in_dim(query_row, q_start, block_item, 0)
        k_part = lax.dynamic_slice_in_dim(k_row, k_start, token_span, 0)
        v_part = lax.dynamic_slice_in_dim(v_row, k_start, token_span, 0)
        scores = (
            jnp.einsum("qhc,khc->hqk", q_part, k_part, preferred_element_type=jnp.float32) * scale
        )
        q_places = q_start + jnp.arange(block_item, dtype=jnp.int32)
        k_places = k_start + jnp.arange(token_span, dtype=jnp.int32)
        starts = lax.dynamic_slice_in_dim(first, q_start, block_item, 0)
        allowed = (k_places[None, :] >= starts[:, None]) & (k_places[None, :] <= q_places[:, None])
        scores = jnp.where(allowed[None], scores, jnp.float32(-1e30))
        top = jnp.max(scores, axis=2, keepdims=True)
        raised = jnp.exp(scores - top)
        weights = (raised / jnp.sum(raised, axis=2, keepdims=True)).astype(jnp.bfloat16)
        return jnp.einsum(
            "hqk,khc->qhc", weights, v_part, preferred_element_type=jnp.float32
        ).astype(jnp.bfloat16)

    block_list = lax.map(single_block, jnp.arange(row_len // block_item, dtype=jnp.int32))
    return block_list.reshape(row_len, query_row.shape[1], query_row.shape[2])


def body(queries, key_states, value_vectors, hypothesis_lengths, join_weight):
    rows, piece, width = (queries.shape[1], queries.shape[2], queries.shape[3])
    devices = lax.axis_size("seq")
    groups = devices // rows
    head_width = width // ATTENTION_HEADS
    pair = width // groups
    heads_here = pair // head_width
    row_bits = rows.bit_length() - 1
    place = lax.axis_index("seq")
    row = place % rows
    row_len = devices * piece

    def regroup(states):
        states = states.reshape(rows, piece, groups, pair)
        return jnp.transpose(states, (2, 0, 1, 3)).reshape(groups * rows, piece, pair)

    q_all, k_all, v_all = (
        lax.all_to_all(regroup(queries[0]), "seq", split_axis=0, concat_axis=1, tiled=True),
        lax.all_to_all(regroup(key_states[0]), "seq", split_axis=0, concat_axis=1, tiled=True),
        lax.all_to_all(regroup(value_vectors[0]), "seq", split_axis=0, concat_axis=1, tiled=True),
    )
    block_rows = join_weight
    for bit in range(row_bits):
        partner = swapped(block_rows, "seq", bit)
        lower = place // 2**bit % 2 == 0
        block_rows = jnp.where(
            lower,
            jnp.concatenate([block_rows, partner], 0),
            jnp.concatenate([partner, block_rows], 0),
        )
    length_list = lax.dynamic_index_in_dim(hypothesis_lengths, row, 0, keepdims=False)
    first, mirror = hypothesis_tables(length_list, row_len)
    array_shape = (row_len, heads_here, head_width)
    context_vectors = attend_group(
        q_all.reshape(array_shape), k_all.reshape(array_shape), v_all.reshape(array_shape), first
    )
    other = swapped(context_vectors, "dir", 0)
    side = lax.axis_index("dir")
    left_side = jnp.where(side == 0, context_vectors, other)
    right_side = jnp.where(side == 0, other, context_vectors)
    right_side = jnp.take(right_side, mirror, axis=0)
    feature_rows = jnp.stack([left_side, right_side], axis=2).reshape(row_len, 2 * pair)
    columns = block_rows.shape[2]
    partial_value = jnp.dot(
        feature_rows, block_rows.reshape(2 * pair, 2 * columns), preferred_element_type=jnp.float32
    ).astype(jnp.bfloat16)
    arrived = lax.all_to_all(
        partial_value.reshape(devices, piece, 2 * columns),
        "seq",
        split_axis=0,
        concat_axis=0,
        tiled=True,
    )
    totals = jnp.sum(arrived.reshape(groups, rows, piece, 2 * columns).astype(jnp.float32), axis=0)
    joined = jax.nn.silu(totals[..., :columns]) * totals[..., columns:]
    return joined.astype(jnp.bfloat16)


def pair_kernel(
    geometry, lengths_ref, q_ref, k_ref, v_ref, weight_ref, out_ref,
    states, queries_up, raw, own, up_from, up_into, down_from, down_into,
    own_stats, up_stats_from, up_stats_into, down_stats_from, down_stats_into,
    weights, feats, sums, partials, arrived, own_moves, up_moves, down_moves, own_bias, up_bias,
    send_sem, recv_sem, local_sem, qsend_sem, qrecv_sem, usend_sem, urecv_sem, dsend_sem, drecv_sem,
    wsend_sem, wrecv_sem, wlocal_sem, csend_sem, crecv_sem, psend_sem, precv_sem,
):
    planes, rows, members, piece, head_width, chunks, halves = geometry
    side = lax.axis_index("dir")
    me = lax.axis_index("seq")
    plane, member = lax.div(me, members), lax.rem(me, members)
    wide = 2 * head_width
    span = members * piece
    scale = 1.0 / math.sqrt(head_width)
    has_up, has_down = plane < planes - 1, plane > 0

    def at(peer):
        return {"device_id": (side, peer), "device_id_type": pl.DeviceIdType.MESH}

    def beside(step):
        return at(plane * members + lax.rem(member + step, members))

    above, below = at(me + members), at(me - members)
    across = {"device_id": (1 - side, me), "device_id_type": pl.DeviceIdType.MESH}

    barrier = pltpu.get_barrier_semaphore()
    for step in range(1, members):
        pl.semaphore_signal(barrier, inc=1, **beside(step))
    pl.semaphore_signal(barrier, inc=1, **across)

    @pl.when(has_up)
    def _():
        pl.semaphore_signal(barrier, inc=1, **above)

    @pl.when(has_down)
    def _():
        pl.semaphore_signal(barrier, inc=1, **below)

    pl.semaphore_wait(barrier, members + jnp.where(has_up, 1, 0) + jnp.where(has_down, 1, 0))

    def weight_copy(shard, half, source, way, target):
        return pltpu.make_async_remote_copy(
            src_ref=source,
            dst_ref=weights.at[shard, half],
            send_sem=wsend_sem.at[way, shard, half],
            recv_sem=wrecv_sem.at[shard, half],
            **target,
        )

    def input_column(chunk, owner):
        return pl.ds(pl.multiple_of((chunk * members + owner) * wide, wide), wide)

    def landing(chunk, index):
        return states.at[chunk, index, :, pl.ds(pl.multiple_of(member * piece, piece), piece), :]

    def send_chunk(chunk):
        for step in range(1, members):
            owner = lax.rem(member + step, members)
            for index, ref in enumerate((q_ref, k_ref, v_ref)):
                pltpu.make_async_remote_copy(
                    src_ref=ref.at[0, :, :, input_column(chunk, owner)],
                    dst_ref=landing(chunk, index),
                    send_sem=send_sem.at[chunk],
                    recv_sem=recv_sem.at[chunk],
                    **beside(step),
                ).start()
        for index, ref in enumerate((q_ref, k_ref, v_ref)):
            pltpu.make_async_copy(
                ref.at[0, :, :, input_column(chunk, member)], landing(chunk, index), local_sem.at[chunk]
            ).start()

    def send_own_weights(half):
        @pl.when(has_up)
        def _():
            weight_copy(plane, half, weight_ref.at[half], 0, above).start()

        @pl.when(has_down)
        def _():
            weight_copy(plane, half, weight_ref.at[half], 1, below).start()

    def send_first(chunk, carry):
        send_chunk(chunk)
        send_own_weights(chunk)
        return carry

    lax.fori_loop(0, halves, send_first, 0)

    own_weights = pltpu.make_async_copy(weight_ref, weights.at[plane], wlocal_sem)
    own_weights.start()

    def relay_weights(step, half):
        @pl.when(plane - step >= 0)
        def _():
            shard = weights.at[plane - step, half]
            pltpu.make_async_copy(shard, shard, wrecv_sem.at[plane - step, half]).wait()

            @pl.when(has_up)
            def _():
                weight_copy(plane - step, half, shard, 0, above).start()

        @pl.when(plane + step < planes)
        def _():
            shard = weights.at[plane + step, half]
            pltpu.make_async_copy(shard, shard, wrecv_sem.at[plane + step, half]).wait()

            @pl.when(has_down)
            def _():
                weight_copy(plane + step, half, shard, 1, below).start()

    @pl.when(jnp.logical_not(has_up))
    def _():
        queries_up[...] = jnp.zeros_like(queries_up)

    @pl.when(jnp.logical_not(has_down))
    def _():
        up_into[...] = jnp.zeros_like(up_into)
        up_stats_into[...] = jnp.zeros_like(up_stats_into)

    gets_down = jnp.logical_and(has_up, side == 1)
    gives_down = jnp.logical_and(has_down, side == 1)

    @pl.when(jnp.logical_not(gets_down))
    def _():
        down_into[...] = jnp.zeros_like(down_into)
        down_stats_into[...] = jnp.zeros_like(down_stats_into)

    slots = lengths_ref.shape[1]
    before = lax.broadcasted_iota(jnp.int32, (slots, slots), 0)
    after = lax.broadcasted_iota(jnp.int32, (slots, slots), 1)
    lengths = lengths_ref[...].astype(jnp.float32)
    all_ends = jnp.dot(
        lengths.astype(jnp.bfloat16),
        jnp.where(before <= after, 1.0, 0.0).astype(jnp.bfloat16),
        preferred_element_type=jnp.float32,
    )
    base = plane * span
    far = 4 * planes * span

    def places_of(row, shift):
        ends = all_ends[row : row + 1].astype(jnp.int32)
        starts = ends - lengths_ref[row : row + 1]
        wide_places = base + shift + lax.broadcasted_iota(jnp.int32, (span, slots), 0)
        inside = (wide_places >= starts) & (wide_places < ends)
        place = base + shift + lax.broadcasted_iota(jnp.int32, (span, 1), 0)
        first = jnp.sum(jnp.where(inside, starts, 0), axis=1, keepdims=True)
        last = jnp.sum(jnp.where(inside, ends, 0), axis=1, keepdims=True) - 1
        return first - base, place - base, first + last - place - base

    k_places = lax.broadcasted_iota(jnp.int32, (span, span), 1)
    q_places = lax.broadcasted_iota(jnp.int32, (span, span), 0)
    places = lax.broadcasted_iota(jnp.int32, (span, 2 * span), 1)
    for row in range(rows):
        first, place, mirror = places_of(row, 0)
        allowed = (k_places >= first) & (k_places <= q_places)
        own_bias[row] = jnp.where(allowed, jnp.float32(0), jnp.float32(-1e30))
        source = jnp.where(side == 0, place, mirror)
        own_moves[row] = jnp.where(places == source, 1.0, 0.0).astype(jnp.bfloat16)
        first, place, mirror = places_of(row, span)
        first = jnp.where(has_up, first, far)
        up_bias[row] = jnp.where(k_places >= first, jnp.float32(0), jnp.float32(-1e30))
        source = jnp.where(side == 0, place, mirror)
        up_moves[row] = jnp.where(places == source, 1.0, 0.0).astype(jnp.bfloat16)
        first, place, mirror = places_of(row, -span)
        source = jnp.where(gives_down, mirror, far)
        down_moves[row] = jnp.where(k_places == source, 1.0, 0.0).astype(jnp.bfloat16)

    def attend(chunk, part, q_of, bias_ref):
        reach = span // 2

        def attend_row(row, inner):
            lane = lax.broadcasted_iota(jnp.int32, (reach, head_width), 1) - row * 8
            mine = (lane >= 0) & (lane < 6)
            for half in range(2):
                at_rows = slice(half * reach, (half + 1) * reach)
                keys = slice(0, (half + 1) * reach) if part == 0 else slice(half * reach, span)
                placed = slice(part * span + half * reach, part * span + (half + 1) * reach)
                tops, totals = [], []
                for head in range(2):
                    lanes = slice(head * head_width, (head + 1) * head_width)
                    scores = lax.dot_general(
                        q_of(row, at_rows, lanes),
                        states[chunk, 1, row, keys, lanes],
                        (((1,), (1,)), ((), ())),
                        preferred_element_type=jnp.float32,
                    )
                    scores = scores * scale + bias_ref[row, at_rows, keys]
                    top = jnp.max(scores, axis=1, keepdims=True)
                    raised = jnp.exp(scores - top)
                    total = jnp.sum(raised, axis=1, keepdims=True)
                    raw[chunk, row, placed, lanes] = jnp.dot(
                        (raised * (1.0 / total)).astype(jnp.bfloat16),
                        states[chunk, 2, row, keys, lanes],
                        preferred_element_type=jnp.float32,
                    ).astype(jnp.bfloat16)
                    tops.append(top)
                    totals.append(total)
                level = jnp.where(lane >= 3, tops[1], tops[0]) + jnp.log(
                    jnp.where(lane >= 3, totals[1], totals[0])
                )
                high = level.astype(jnp.bfloat16).astype(jnp.float32)
                level = level - high
                middle = level.astype(jnp.bfloat16).astype(jnp.float32)
                low = level - middle
                digits = jnp.where(
                    (lane == 0) | (lane == 3), high, jnp.where((lane == 1) | (lane == 4), middle, low)
                )
                digits = jnp.where(mine, digits, jnp.where(lane == 6, 1.0, 0.0))
                raw[chunk, row, placed, wide:] = digits.astype(jnp.bfloat16)
            return inner

        lax.fori_loop(0, rows, attend_row, 0)

    def query_copy(chunk):
        return pltpu.make_async_remote_copy(
            src_ref=states.at[chunk, 0],
            dst_ref=queries_up.at[chunk],
            send_sem=qsend_sem.at[chunk],
            recv_sem=qrecv_sem.at[chunk],
            **below,
        )

    def context_copies(chunk, sources, targets, sends, receives, device):
        return [
            pltpu.make_async_remote_copy(
                src_ref=source.at[chunk],
                dst_ref=target.at[chunk],
                send_sem=sends.at[chunk, index],
                recv_sem=receives.at[chunk, index],
                **device,
            )
            for index, (source, target) in enumerate(zip(sources, targets))
        ]

    def up_copies(chunk):
        return context_copies(
            chunk, (up_from, up_stats_from), (up_into, up_stats_into), usend_sem, urecv_sem, above
        )

    def down_copies(chunk):
        return context_copies(
            chunk, (down_from, down_stats_from), (down_into, down_stats_into), dsend_sem, drecv_sem, below
        )

    def wait_for(refs, sems, chunk):
        for index, ref in enumerate(refs):
            pltpu.make_async_copy(ref.at[chunk], ref.at[chunk], sems.at[chunk, index]).wait()

    def exchange(chunk, head):
        column = pl.multiple_of((2 * head + side) * head_width, head_width)
        there = feats.at[chunk, :, :, pl.ds(column, head_width)]
        return pltpu.make_async_remote_copy(
            src_ref=there,
            dst_ref=there,
            send_sem=csend_sem.at[chunk, head],
            recv_sem=crecv_sem.at[chunk, head],
            **across,
        )

    def local_stage(chunk):
        others = states.at[chunk, :, :, pl.ds(0, span - piece), :]
        pltpu.make_async_copy(others, others, recv_sem.at[chunk]).wait()
        mine = states.at[chunk, :, :, pl.ds(0, piece), :]
        pltpu.make_async_copy(mine, mine, local_sem.at[chunk]).wait()

        @pl.when(has_down)
        def _():
            query_copy(chunk).start()

        @pl.when(chunk + halves < chunks)
        def _():
            send_chunk(chunk + halves)

        attend(chunk, 0, lambda row, at_rows, lanes: states[chunk, 0, row, at_rows, lanes], own_bias)

    def moved_part(moves, source, chunk, row, target):
        moved = jnp.dot(moves[row], source, preferred_element_type=jnp.float32)
        target[chunk, row] = moved[:, :wide].astype(jnp.bfloat16)
        return moved[:, wide:]

    def cross_stage(chunk):
        @pl.when(has_up)
        def _():
            pltpu.make_async_copy(
                queries_up.at[chunk], queries_up.at[chunk], qrecv_sem.at[chunk]
            ).wait()

        attend(chunk, 1, lambda row, at_rows, lanes: queries_up[chunk, row, at_rows, lanes], up_bias)

        @pl.when(has_up)
        def _():
            stats = 0.0
            for row in range(rows):
                stats = stats + moved_part(up_moves, raw[chunk, row], chunk, row, up_from)
            up_stats_from[chunk] = stats.astype(jnp.bfloat16)
            for copy in up_copies(chunk):
                copy.start()

        @pl.when(gives_down)
        def _():
            stats = 0.0
            for row in range(rows):
                stats = stats + moved_part(down_moves, raw[chunk, row, :span], chunk, row, down_from)
            down_stats_from[chunk] = stats.astype(jnp.bfloat16)
            for copy in down_copies(chunk):
                copy.start()

        stats = 0.0
        for row in range(rows):
            stats = stats + moved_part(own_moves, raw[chunk, row], chunk, row, own)
        own_stats[chunk] = stats.astype(jnp.bfloat16)

    def merge_stage(chunk):
        @pl.when(has_down)
        def _():
            wait_for((up_into, up_stats_into), urecv_sem, chunk)

        @pl.when(gets_down)
        def _():
            wait_for((down_into, down_stats_into), drecv_sem, chunk)

        lane_in = lax.broadcasted_iota(jnp.int32, (head_width, head_width), 0)
        lane_out = lax.broadcasted_iota(jnp.int32, (head_width, head_width), 1)
        same_row = lane_in // 8 == lane_out // 8
        digit_in, digit_out = lane_in % 8, lane_out % 8
        same_head = (digit_in < 6) & ((digit_in >= 3) == (digit_out >= 3))
        gather = jnp.where(same_row & same_head, 1.0, 0.0).astype(jnp.bfloat16)
        marks = jnp.where(same_row & (digit_in == 6), 1.0, 0.0).astype(jnp.bfloat16)
        levels = []
        for ref in (own_stats, up_stats_into, down_stats_into):
            stat = ref[chunk]
            level = jnp.dot(stat, gather, preferred_element_type=jnp.float32)
            present = jnp.dot(stat, marks, preferred_element_type=jnp.float32)
            levels.append(jnp.where(present > 0.5, level, jnp.float32(-3e30)))
        top = jnp.maximum(jnp.maximum(levels[0], levels[1]), levels[2])
        shares = [jnp.exp(level - top) for level in levels]
        norm = 1.0 / (shares[0] + shares[1] + shares[2])
        shares = [share * norm for share in shares]
        for row in range(rows):
            for head in range(2):
                lanes = slice(head * head_width, (head + 1) * head_width)
                lane = row * 8 + head * 3
                value = 0.0
                for part, share in zip((own, up_into, down_into), shares):
                    value = value + part[chunk, row, :, lanes].astype(jnp.float32) * share[:, lane : lane + 1]
                value = value.astype(jnp.bfloat16)
                column = pl.multiple_of((2 * head + side) * head_width, head_width)
                for owner in range(members):
                    feats[chunk, owner, row * piece : (row + 1) * piece, pl.ds(column, head_width)] = value[
                        owner * piece : (owner + 1) * piece
                    ]
        for head in range(2):
            exchange(chunk, head).start()

    def stage(step, carry):
        @pl.when(step < chunks)
        def _():
            local_stage(step)

        @pl.when(jnp.logical_and(step >= 1, step <= chunks))
        def _():
            cross_stage(step - 1)

        for late in range(1, planes - 1):

            @pl.when(step == 2 * late)
            def _():
                for half in range(halves):
                    relay_weights(late, half)

        @pl.when(step >= 2)
        def _():
            merge_stage(step - 2)

        return carry

    lax.fori_loop(0, chunks + 2, stage, 0)

    own_weights.wait()

    def arrive(chunk, carry):
        for head in range(2):
            column = pl.multiple_of((2 * head + 1 - side) * head_width, head_width)
            there = feats.at[chunk, :, :, pl.ds(column, head_width)]
            pltpu.make_async_copy(there, there, crecv_sem.at[chunk, head]).wait()
        return carry

    lax.fori_loop(0, chunks, arrive, 0)

    low_half = plane < planes // 2
    last = jnp.where(low_half, chunks - 1, 0)

    def join_early(owner, carry):
        for half in range(halves):
            total = 0.0
            for step in range(chunks - 1):
                chunk = jnp.where(low_half, step, chunks - 1 - step)
                total = total + jnp.dot(
                    feats[chunk, owner], weights[chunk, half], preferred_element_type=jnp.float32
                )
            sums[half, owner] = total
        return carry

    lax.fori_loop(0, members, join_early, 0)

    def partial_copy(half, owner):
        return pltpu.make_async_remote_copy(
            src_ref=partials.at[half, owner],
            dst_ref=arrived.at[half, member],
            send_sem=psend_sem.at[half],
            recv_sem=precv_sem.at[half],
            **at(plane * members + owner),
        )

    def join_half(half, carry):
        relay_weights(planes - 1, half)

        def join_last(step, inner):
            owner = lax.rem(member + 1 + step, members)
            total = sums[half, owner] + jnp.dot(
                feats[last, owner], weights[last, half], preferred_element_type=jnp.float32
            )
            partials[half, owner] = total.astype(jnp.bfloat16)

            @pl.when(step < members - 1)
            def _():
                partial_copy(half, owner).start()

            return inner

        lax.fori_loop(0, members, join_last, 0)
        arrived[half, member] = partials[half, member]
        return carry

    lax.fori_loop(0, halves, join_half, 0)
    columns = out_ref.shape[2] // halves
    for half in range(halves):
        incoming = arrived.at[half, pl.ds(0, members - 1)]
        pltpu.make_async_copy(incoming, incoming, precv_sem.at[half]).wait()
        for row in range(rows):
            total = 0.0
            for source in range(members):
                total = total + arrived[half, source, row * piece : (row + 1) * piece, :].astype(
                    jnp.float32
                )
            gate, up = total[:, :columns], total[:, columns:]
            out_ref[row, :, half * columns : (half + 1) * columns] = (
                gate / (1.0 + jnp.exp(-gate)) * up
            ).astype(jnp.bfloat16)

    def finish(chunk, carry):
        others = states.at[chunk, :, :, pl.ds(0, span - piece), :]
        pltpu.make_async_copy(others, others, send_sem.at[chunk]).wait()
        for head in range(2):
            exchange(chunk, head).wait_send()

        @pl.when(has_up)
        def _():
            for copy in up_copies(chunk):
                copy.wait_send()

        @pl.when(has_down)
        def _():
            query_copy(chunk).wait_send()

        @pl.when(gives_down)
        def _():
            for copy in down_copies(chunk):
                copy.wait_send()

        return carry

    lax.fori_loop(0, chunks, finish, 0)
    for step in range(planes):

        @pl.when(jnp.logical_and(has_up, plane - step >= 0))
        def _():
            for half in range(halves):
                weight_copy(plane - step, half, weights.at[plane - step, half], 0, above).wait_send()

        @pl.when(jnp.logical_and(has_down, plane + step < planes))
        def _():
            for half in range(halves):
                weight_copy(plane + step, half, weights.at[plane + step, half], 1, below).wait_send()

    for half in range(halves):
        incoming = arrived.at[half, pl.ds(0, members - 1)]
        pltpu.make_async_copy(incoming, incoming, psend_sem.at[half]).wait()


def fused_body(queries, key_states, value_vectors, hypothesis_lengths, join_weight):
    rows, piece, width = (queries.shape[1], queries.shape[2], queries.shape[3])
    devices = lax.axis_size("seq")
    planes, members = devices // PACKED_ROWS, PACKED_ROWS
    head_width = width // ATTENTION_HEADS
    wide = 2 * head_width
    chunks = width // (members * wide)
    span = members * piece
    halves = 2
    weight_rows, _, columns = join_weight.shape
    part = columns // halves
    by_halves = jnp.transpose(join_weight.reshape(weight_rows, 2, halves, part), (2, 0, 1, 3))
    geometry = (planes, rows, members, piece, head_width, chunks, halves)

    def vmem(*shape):
        return pltpu.VMEM(shape, jnp.bfloat16)

    dma = pltpu.SemaphoreType.DMA
    context = (chunks, rows, span, wide)
    stats = (chunks, span, head_width)
    return pl.pallas_call(
        functools.partial(pair_kernel, geometry),
        out_shape=jax.ShapeDtypeStruct((rows, piece, columns), jnp.bfloat16),
        in_specs=[pl.BlockSpec(memory_space=pltpu.VMEM)] + [pl.BlockSpec(memory_space=pl.ANY)] * 4,
        out_specs=pl.BlockSpec(memory_space=pltpu.VMEM),
        scratch_shapes=[
            vmem(chunks, 3, rows, span, wide),
            vmem(*context),
            vmem(chunks, rows, 2 * span, wide + head_width),
            *[vmem(*context)] * 5,
            *[vmem(*stats)] * 5,
            vmem(planes, halves, weight_rows, 2 * part),
            vmem(chunks, members, rows * piece, 2 * wide),
            pltpu.VMEM((halves, members, rows * piece, 2 * part), jnp.float32),
            vmem(halves, members, rows * piece, 2 * part),
            vmem(halves, members, rows * piece, 2 * part),
            vmem(rows, span, 2 * span),
            vmem(rows, span, 2 * span),
            vmem(rows, span, span),
            pltpu.VMEM((rows, span, span), jnp.float32),
            pltpu.VMEM((rows, span, span), jnp.float32),
            dma((chunks,)),
            dma((chunks,)),
            dma((chunks,)),
            dma((chunks,)),
            dma((chunks,)),
            dma((chunks, 2)),
            dma((chunks, 2)),
            dma((chunks, 2)),
            dma((chunks, 2)),
            dma((2, planes, halves)),
            dma((planes, halves)),
            dma,
            dma((chunks, 2)),
            dma((chunks, 2)),
            dma((halves,)),
            dma((halves,)),
        ],
        compiler_params=pltpu.CompilerParams(
            collective_id=0, has_side_effects=True, vmem_limit_bytes=60 * 1024 * 1024
        ),
    )(
        hypothesis_lengths,
        queries,
        key_states,
        value_vectors,
        by_halves.reshape(halves, weight_rows, 2 * part),
    )


def fits_kernel(mesh):
    planes = mesh.shape["seq"] // PACKED_ROWS
    return ATTENTION_HEADS // planes == 2 * PACKED_ROWS


def solution(mesh):
    return jax.shard_map(
        fused_body if fits_kernel(mesh) else body,
        mesh=mesh,
        in_specs=(
            P("dir", None, "seq", None),
            P("dir", None, "seq", None),
            P("dir", None, "seq", None),
            P(),
            P("seq", None, "dir"),
        ),
        out_specs=P(None, "seq", "dir"),
        check_vma=False,
    )
```

```python
import functools
import math

import jax
import jax.numpy as jnp
from jax import lax
from jax.experimental import pallas as pl
from jax.experimental.pallas import tpu as pltpu
from jax.sharding import PartitionSpec as P

ATTENTION_HEADS = 32
LONGEST_TOKENS = 256
PACKED_ROWS = 4


def swapped(array, axis, stride):
    return lax.ppermute(array, axis, [(i, i ^ 1 << stride) for i in range(lax.axis_size(axis))])


def hypothesis_tables(length_list, row_len):
    ends = jnp.cumsum(length_list)
    starts = ends - length_list
    places = jnp.arange(row_len, dtype=jnp.int32)
    inside = (places[:, None] >= starts[None, :]) & (places[:, None] < ends[None, :])
    first = jnp.sum(jnp.where(inside, starts[None, :], 0), axis=1)
    after = jnp.sum(jnp.where(inside, ends[None, :], 0), axis=1)
    mirror = first + after - 1 - places
    return (first, mirror)


def attend_group(query_row, k_row, v_row, first):
    row_len = query_row.shape[0]
    block_item = min(512, row_len)
    token_span = min(block_item + LONGEST_TOKENS, row_len)
    scale = 1.0 / math.sqrt(query_row.shape[2])

    def single_block(index):
        q_start = index * block_item
        k_start = jnp.maximum(q_start + block_item - token_span, 0)
        q_part = lax.dynamic_slice_in_dim(query_row, q_start, block_item, 0)
        k_part = lax.dynamic_slice_in_dim(k_row, k_start, token_span, 0)
        v_part = lax.dynamic_slice_in_dim(v_row, k_start, token_span, 0)
        scores = (
            jnp.einsum("qhc,khc->hqk", q_part, k_part, preferred_element_type=jnp.float32) * scale
        )
        q_places = q_start + jnp.arange(block_item, dtype=jnp.int32)
        k_places = k_start + jnp.arange(token_span, dtype=jnp.int32)
        starts = lax.dynamic_slice_in_dim(first, q_start, block_item, 0)
        allowed = (k_places[None, :] >= starts[:, None]) & (k_places[None, :] <= q_places[:, None])
        scores = jnp.where(allowed[None], scores, jnp.float32(-1e30))
        top = jnp.max(scores, axis=2, keepdims=True)
        raised = jnp.exp(scores - top)
        weights = (raised / jnp.sum(raised, axis=2, keepdims=True)).astype(jnp.bfloat16)
        return jnp.einsum(
            "hqk,khc->qhc", weights, v_part, preferred_element_type=jnp.float32
        ).astype(jnp.bfloat16)

    block_list = lax.map(single_block, jnp.arange(row_len // block_item, dtype=jnp.int32))
    return block_list.reshape(row_len, query_row.shape[1], query_row.shape[2])


def body(queries, key_states, value_vectors, hypothesis_lengths, join_weight):
    rows, piece, width = (queries.shape[1], queries.shape[2], queries.shape[3])
    devices = lax.axis_size("seq")
    groups = devices // rows
    head_width = width // ATTENTION_HEADS
    pair = width // groups
    heads_here = pair // head_width
    row_bits = rows.bit_length() - 1
    place = lax.axis_index("seq")
    row = place % rows
    row_len = devices * piece

    def regroup(states):
        states = states.reshape(rows, piece, groups, pair)
        return jnp.transpose(states, (2, 0, 1, 3)).reshape(groups * rows, piece, pair)

    q_all, k_all, v_all = (
        lax.all_to_all(regroup(queries[0]), "seq", split_axis=0, concat_axis=1, tiled=True),
        lax.all_to_all(regroup(key_states[0]), "seq", split_axis=0, concat_axis=1, tiled=True),
        lax.all_to_all(regroup(value_vectors[0]), "seq", split_axis=0, concat_axis=1, tiled=True),
    )
    block_rows = join_weight
    for bit in range(row_bits):
        partner = swapped(block_rows, "seq", bit)
        lower = place // 2**bit % 2 == 0
        block_rows = jnp.where(
            lower,
            jnp.concatenate([block_rows, partner], 0),
            jnp.concatenate([partner, block_rows], 0),
        )
    length_list = lax.dynamic_index_in_dim(hypothesis_lengths, row, 0, keepdims=False)
    first, mirror = hypothesis_tables(length_list, row_len)
    array_shape = (row_len, heads_here, head_width)
    context_vectors = attend_group(
        q_all.reshape(array_shape), k_all.reshape(array_shape), v_all.reshape(array_shape), first
    )
    other = swapped(context_vectors, "dir", 0)
    side = lax.axis_index("dir")
    left_side = jnp.where(side == 0, context_vectors, other)
    right_side = jnp.where(side == 0, other, context_vectors)
    right_side = jnp.take(right_side, mirror, axis=0)
    feature_rows = jnp.stack([left_side, right_side], axis=2).reshape(row_len, 2 * pair)
    columns = block_rows.shape[2]
    partial_value = jnp.dot(
        feature_rows, block_rows.reshape(2 * pair, 2 * columns), preferred_element_type=jnp.float32
    ).astype(jnp.bfloat16)
    arrived = lax.all_to_all(
        partial_value.reshape(devices, piece, 2 * columns),
        "seq",
        split_axis=0,
        concat_axis=0,
        tiled=True,
    )
    totals = jnp.sum(arrived.reshape(groups, rows, piece, 2 * columns).astype(jnp.float32), axis=0)
    joined = jax.nn.silu(totals[..., :columns]) * totals[..., columns:]
    return joined.astype(jnp.bfloat16)


def pair_kernel(
    geometry, lengths_ref, q_ref, k_ref, v_ref, weight_ref, out_ref,
    states, queries_up, raw, own, up_from, up_into, down_from, down_into,
    own_stats, up_stats_from, up_stats_into, down_stats_from, down_stats_into,
    weights, feats, sums, partials, arrived, own_moves, up_moves, down_moves, spread_moves, own_bias, up_bias,
    send_sem, recv_sem, local_sem, qsend_sem, qrecv_sem, usend_sem, urecv_sem, dsend_sem, drecv_sem,
    wsend_sem, wrecv_sem, wlocal_sem, csend_sem, crecv_sem, psend_sem, precv_sem,
):
    planes, rows, members, piece, head_width, chunks, halves = geometry
    side = lax.axis_index("dir")
    me = lax.axis_index("seq")
    plane, member = lax.div(me, members), lax.rem(me, members)
    wide = 2 * head_width
    span = members * piece
    scale = 1.0 / math.sqrt(head_width)
    has_up, has_down = plane < planes - 1, plane > 0

    def at(peer):
        return {"device_id": (side, peer), "device_id_type": pl.DeviceIdType.MESH}

    def beside(step):
        return at(plane * members + lax.rem(member + step, members))

    above, below = at(me + members), at(me - members)
    across = {"device_id": (1 - side, me), "device_id_type": pl.DeviceIdType.MESH}

    barrier = pltpu.get_barrier_semaphore()
    for step in range(1, members):
        pl.semaphore_signal(barrier, inc=1, **beside(step))
    pl.semaphore_signal(barrier, inc=1, **across)

    @pl.when(has_up)
    def _():
        pl.semaphore_signal(barrier, inc=1, **above)

    @pl.when(has_down)
    def _():
        pl.semaphore_signal(barrier, inc=1, **below)

    pl.semaphore_wait(barrier, members + jnp.where(has_up, 1, 0) + jnp.where(has_down, 1, 0))

    def weight_copy(shard, half, source, way, target):
        return pltpu.make_async_remote_copy(
            src_ref=source,
            dst_ref=weights.at[shard, half],
            send_sem=wsend_sem.at[way, shard, half],
            recv_sem=wrecv_sem.at[shard, half],
            **target,
        )

    def input_column(chunk, owner):
        return pl.ds(pl.multiple_of((chunk * members + owner) * wide, wide), wide)

    def landing(chunk, index):
        return states.at[chunk, index, :, pl.ds(pl.multiple_of(member * piece, piece), piece), :]

    def send_chunk(chunk):
        for step in range(1, members):
            owner = lax.rem(member + step, members)
            for index, ref in enumerate((q_ref, k_ref, v_ref)):
                pltpu.make_async_remote_copy(
                    src_ref=ref.at[0, :, :, input_column(chunk, owner)],
                    dst_ref=landing(chunk, index),
                    send_sem=send_sem.at[chunk],
                    recv_sem=recv_sem.at[chunk],
                    **beside(step),
                ).start()
        for index, ref in enumerate((q_ref, k_ref, v_ref)):
            pltpu.make_async_copy(
                ref.at[0, :, :, input_column(chunk, member)], landing(chunk, index), local_sem.at[chunk]
            ).start()

    def send_own_weights(half):
        @pl.when(has_up)
        def _():
            weight_copy(plane, half, weight_ref.at[half], 0, above).start()

        @pl.when(has_down)
        def _():
            weight_copy(plane, half, weight_ref.at[half], 1, below).start()

    def send_first(chunk, carry):
        send_chunk(chunk)
        send_own_weights(chunk)
        return carry

    lax.fori_loop(0, halves, send_first, 0)

    own_weights = pltpu.make_async_copy(weight_ref, weights.at[plane], wlocal_sem)
    own_weights.start()

    def relay_weights(step, half):
        @pl.when(plane - step >= 0)
        def _():
            shard = weights.at[plane - step, half]
            pltpu.make_async_copy(shard, shard, wrecv_sem.at[plane - step, half]).wait()

            @pl.when(has_up)
            def _():
                weight_copy(plane - step, half, shard, 0, above).start()

        @pl.when(plane + step < planes)
        def _():
            shard = weights.at[plane + step, half]
            pltpu.make_async_copy(shard, shard, wrecv_sem.at[plane + step, half]).wait()

            @pl.when(has_down)
            def _():
                weight_copy(plane + step, half, shard, 1, below).start()

    @pl.when(jnp.logical_not(has_up))
    def _():
        queries_up[...] = jnp.zeros_like(queries_up)

    @pl.when(jnp.logical_not(has_down))
    def _():
        up_into[...] = jnp.zeros_like(up_into)
        up_stats_into[...] = jnp.zeros_like(up_stats_into)

    gets_down = jnp.logical_and(has_up, side == 1)
    gives_down = jnp.logical_and(has_down, side == 1)

    @pl.when(jnp.logical_not(gets_down))
    def _():
        down_into[...] = jnp.zeros_like(down_into)
        down_stats_into[...] = jnp.zeros_like(down_stats_into)

    slots = lengths_ref.shape[1]
    before = lax.broadcasted_iota(jnp.int32, (slots, slots), 0)
    after = lax.broadcasted_iota(jnp.int32, (slots, slots), 1)
    lengths = lengths_ref[...].astype(jnp.float32)
    all_ends = jnp.dot(
        lengths.astype(jnp.bfloat16),
        jnp.where(before <= after, 1.0, 0.0).astype(jnp.bfloat16),
        preferred_element_type=jnp.float32,
    )
    base = plane * span
    far = 4 * planes * span

    def places_of(row, shift):
        ends = all_ends[row : row + 1].astype(jnp.int32)
        starts = ends - lengths_ref[row : row + 1]
        wide_places = base + shift + lax.broadcasted_iota(jnp.int32, (span, slots), 0)
        inside = (wide_places >= starts) & (wide_places < ends)
        place = base + shift + lax.broadcasted_iota(jnp.int32, (span, 1), 0)
        first = jnp.sum(jnp.where(inside, starts, 0), axis=1, keepdims=True)
        last = jnp.sum(jnp.where(inside, ends, 0), axis=1, keepdims=True) - 1
        return first - base, place - base, first + last - place - base

    k_places = lax.broadcasted_iota(jnp.int32, (span, span), 1)
    q_places = lax.broadcasted_iota(jnp.int32, (span, span), 0)
    places = lax.broadcasted_iota(jnp.int32, (span, 2 * span), 1)
    for row in range(rows):
        first, place, mirror = places_of(row, 0)
        allowed = (k_places >= first) & (k_places <= q_places)
        own_bias[row] = jnp.where(allowed, jnp.float32(0), jnp.float32(-1e30))
        source = jnp.where(side == 0, place, mirror)
        own_moves[row] = jnp.where(places == source, 1.0, 0.0).astype(jnp.bfloat16)
        slot = lax.broadcasted_iota(jnp.int32, (span // 2, span), 0)
        final = mirror[0:1] - first[0:1]
        given = (slot < -first[0:1]) & (k_places[: span // 2] == final - slot)
        down_moves[row] = jnp.where(given, 1.0, 0.0).astype(jnp.bfloat16)
        slot = lax.broadcasted_iota(jnp.int32, (span, span // 2), 1)
        taken = (mirror >= span) & (slot == place - first)
        spread_moves[row] = jnp.where(taken, 1.0, 0.0).astype(jnp.bfloat16)
        first, place, mirror = places_of(row, span)
        first = jnp.where(has_up, first, far)
        up_bias[row] = jnp.where(k_places >= first, jnp.float32(0), jnp.float32(-1e30))
        source = jnp.where(side == 0, place, mirror)
        up_moves[row] = jnp.where(places == source, 1.0, 0.0).astype(jnp.bfloat16)

    def attend(chunk, part, q_of, bias_ref):
        reach = span // 2

        def attend_row(row, inner):
            lane = lax.broadcasted_iota(jnp.int32, (reach, head_width), 1) - row * 8
            mine = (lane >= 0) & (lane < 6)
            for half in range(2):
                at_rows = slice(half * reach, (half + 1) * reach)
                keys = slice(0, (half + 1) * reach) if part == 0 else slice(half * reach, span)
                placed = slice(part * span + half * reach, part * span + (half + 1) * reach)
                tops, totals = [], []
                for head in range(2):
                    lanes = slice(head * head_width, (head + 1) * head_width)
                    scores = lax.dot_general(
                        q_of(row, at_rows, lanes),
                        states[chunk, 1, row, keys, lanes],
                        (((1,), (1,)), ((), ())),
                        preferred_element_type=jnp.float32,
                    )
                    scores = scores * scale + bias_ref[row, at_rows, keys]
                    top = jnp.max(scores, axis=1, keepdims=True)
                    raised = jnp.exp(scores - top)
                    total = jnp.sum(raised, axis=1, keepdims=True)
                    raw[chunk, row, placed, lanes] = jnp.dot(
                        (raised * (1.0 / total)).astype(jnp.bfloat16),
                        states[chunk, 2, row, keys, lanes],
                        preferred_element_type=jnp.float32,
                    ).astype(jnp.bfloat16)
                    tops.append(top)
                    totals.append(total)
                level = jnp.where(lane >= 3, tops[1], tops[0]) + jnp.log(
                    jnp.where(lane >= 3, totals[1], totals[0])
                )
                high = level.astype(jnp.bfloat16).astype(jnp.float32)
                level = level - high
                middle = level.astype(jnp.bfloat16).astype(jnp.float32)
                low = level - middle
                digits = jnp.where(
                    (lane == 0) | (lane == 3), high, jnp.where((lane == 1) | (lane == 4), middle, low)
                )
                digits = jnp.where(mine, digits, jnp.where(lane == 6, 1.0, 0.0))
                raw[chunk, row, placed, wide:] = digits.astype(jnp.bfloat16)
            return inner

        lax.fori_loop(0, rows, attend_row, 0)

    def query_copy(chunk):
        return pltpu.make_async_remote_copy(
            src_ref=states.at[chunk, 0],
            dst_ref=queries_up.at[chunk],
            send_sem=qsend_sem.at[chunk],
            recv_sem=qrecv_sem.at[chunk],
            **below,
        )

    def context_copies(chunk, sources, targets, sends, receives, device):
        return [
            pltpu.make_async_remote_copy(
                src_ref=source.at[chunk],
                dst_ref=target.at[chunk],
                send_sem=sends.at[chunk, index],
                recv_sem=receives.at[chunk, index],
                **device,
            )
            for index, (source, target) in enumerate(zip(sources, targets))
        ]

    def up_copies(chunk):
        return context_copies(
            chunk, (up_from, up_stats_from), (up_into, up_stats_into), usend_sem, urecv_sem, above
        )

    def down_copies(chunk):
        return context_copies(
            chunk, (down_from, down_stats_from), (down_into, down_stats_into), dsend_sem, drecv_sem, below
        )

    def wait_for(refs, sems, chunk):
        for index, ref in enumerate(refs):
            pltpu.make_async_copy(ref.at[chunk], ref.at[chunk], sems.at[chunk, index]).wait()

    def exchange(chunk, head):
        column = pl.multiple_of((2 * head + side) * head_width, head_width)
        there = feats.at[chunk, :, :, pl.ds(column, head_width)]
        return pltpu.make_async_remote_copy(
            src_ref=there,
            dst_ref=there,
            send_sem=csend_sem.at[chunk, head],
            recv_sem=crecv_sem.at[chunk, head],
            **across,
        )

    def local_stage(chunk):
        others = states.at[chunk, :, :, pl.ds(0, span - piece), :]
        pltpu.make_async_copy(others, others, recv_sem.at[chunk]).wait()
        mine = states.at[chunk, :, :, pl.ds(0, piece), :]
        pltpu.make_async_copy(mine, mine, local_sem.at[chunk]).wait()

        @pl.when(has_down)
        def _():
            query_copy(chunk).start()

        @pl.when(chunk + halves < chunks)
        def _():
            send_chunk(chunk + halves)

        attend(chunk, 0, lambda row, at_rows, lanes: states[chunk, 0, row, at_rows, lanes], own_bias)

    def moved_part(moves, source, chunk, row, target):
        moved = jnp.dot(moves[row], source, preferred_element_type=jnp.float32)
        target[chunk, row] = moved[:, :wide].astype(jnp.bfloat16)
        return moved[:, wide:]

    def cross_stage(chunk):
        @pl.when(has_up)
        def _():
            pltpu.make_async_copy(
                queries_up.at[chunk], queries_up.at[chunk], qrecv_sem.at[chunk]
            ).wait()

        attend(chunk, 1, lambda row, at_rows, lanes: queries_up[chunk, row, at_rows, lanes], up_bias)

        @pl.when(has_up)
        def _():
            stats = 0.0
            for row in range(rows):
                stats = stats + moved_part(up_moves, raw[chunk, row], chunk, row, up_from)
            up_stats_from[chunk] = stats.astype(jnp.bfloat16)
            for copy in up_copies(chunk):
                copy.start()

        @pl.when(gives_down)
        def _():
            stats = 0.0
            for row in range(rows):
                stats = stats + moved_part(down_moves, raw[chunk, row, :span], chunk, row, down_from)
            down_stats_from[chunk] = stats.astype(jnp.bfloat16)
            for copy in down_copies(chunk):
                copy.start()

        stats = 0.0
        for row in range(rows):
            stats = stats + moved_part(own_moves, raw[chunk, row], chunk, row, own)
        own_stats[chunk] = stats.astype(jnp.bfloat16)

    def merge_stage(chunk):
        @pl.when(has_down)
        def _():
            wait_for((up_into, up_stats_into), urecv_sem, chunk)

        @pl.when(gets_down)
        def _():
            wait_for((down_into, down_stats_into), drecv_sem, chunk)

        lane_in = lax.broadcasted_iota(jnp.int32, (head_width, head_width), 0)
        lane_out = lax.broadcasted_iota(jnp.int32, (head_width, head_width), 1)
        same_row = lane_in // 8 == lane_out // 8
        digit_in, digit_out = lane_in % 8, lane_out % 8
        same_head = (digit_in < 6) & ((digit_in >= 3) == (digit_out >= 3))
        gather = jnp.where(same_row & same_head, 1.0, 0.0).astype(jnp.bfloat16)
        marks = jnp.where(same_row & (digit_in == 6), 1.0, 0.0).astype(jnp.bfloat16)
        row_lane = lax.broadcasted_iota(jnp.int32, (span, head_width), 1) // 8
        down_stats = 0.0
        for row in range(rows):
            spread = jnp.dot(
                spread_moves[row], down_stats_into[chunk], preferred_element_type=jnp.float32
            )
            down_stats = down_stats + jnp.where(row_lane == row, spread, 0.0)
        levels = []
        for stat in (own_stats[chunk], up_stats_into[chunk], down_stats.astype(jnp.bfloat16)):
            level = jnp.dot(stat, gather, preferred_element_type=jnp.float32)
            present = jnp.dot(stat, marks, preferred_element_type=jnp.float32)
            levels.append(jnp.where(present > 0.5, level, jnp.float32(-3e30)))
        top = jnp.maximum(jnp.maximum(levels[0], levels[1]), levels[2])
        shares = [jnp.exp(level - top) for level in levels]
        norm = 1.0 / (shares[0] + shares[1] + shares[2])
        shares = [share * norm for share in shares]
        for row in range(rows):
            spread = jnp.dot(
                spread_moves[row], down_into[chunk, row], preferred_element_type=jnp.float32
            )
            for head in range(2):
                lanes = slice(head * head_width, (head + 1) * head_width)
                lane = row * 8 + head * 3
                value = spread[:, lanes] * shares[2][:, lane : lane + 1]
                for part, share in zip((own, up_into), shares):
                    value = value + part[chunk, row, :, lanes].astype(jnp.float32) * share[:, lane : lane + 1]
                value = value.astype(jnp.bfloat16)
                column = pl.multiple_of((2 * head + side) * head_width, head_width)
                for owner in range(members):
                    feats[chunk, owner, row * piece : (row + 1) * piece, pl.ds(column, head_width)] = value[
                        owner * piece : (owner + 1) * piece
                    ]
        for head in range(2):
            exchange(chunk, head).start()

    def stage(step, carry):
        @pl.when(step < chunks)
        def _():
            local_stage(step)

        @pl.when(jnp.logical_and(step >= 1, step <= chunks))
        def _():
            cross_stage(step - 1)

        for late in range(1, planes - 1):

            @pl.when(step == 2 * late)
            def _():
                for half in range(halves):
                    relay_weights(late, half)

        @pl.when(step >= 2)
        def _():
            merge_stage(step - 2)

        return carry

    lax.fori_loop(0, chunks + 2, stage, 0)

    own_weights.wait()

    def arrive(chunk, carry):
        for head in range(2):
            column = pl.multiple_of((2 * head + 1 - side) * head_width, head_width)
            there = feats.at[chunk, :, :, pl.ds(column, head_width)]
            pltpu.make_async_copy(there, there, crecv_sem.at[chunk, head]).wait()
        return carry

    lax.fori_loop(0, chunks, arrive, 0)

    low_half = plane < planes // 2
    last = jnp.where(low_half, chunks - 1, 0)

    def join_early(owner, carry):
        for half in range(halves):
            total = 0.0
            for step in range(chunks - 1):
                chunk = jnp.where(low_half, step, chunks - 1 - step)
                total = total + jnp.dot(
                    feats[chunk, owner], weights[chunk, half], preferred_element_type=jnp.float32
                )
            sums[half, owner] = total
        return carry

    lax.fori_loop(0, members, join_early, 0)

    def partial_copy(half, owner):
        return pltpu.make_async_remote_copy(
            src_ref=partials.at[half, owner],
            dst_ref=arrived.at[half, member],
            send_sem=psend_sem.at[half],
            recv_sem=precv_sem.at[half],
            **at(plane * members + owner),
        )

    def join_half(half, carry):
        relay_weights(planes - 1, half)

        def join_last(step, inner):
            owner = lax.rem(member + 1 + step, members)
            total = sums[half, owner] + jnp.dot(
                feats[last, owner], weights[last, half], preferred_element_type=jnp.float32
            )
            partials[half, owner] = total.astype(jnp.bfloat16)

            @pl.when(step < members - 1)
            def _():
                partial_copy(half, owner).start()

            return inner

        lax.fori_loop(0, members, join_last, 0)
        arrived[half, member] = partials[half, member]
        return carry

    lax.fori_loop(0, halves, join_half, 0)
    columns = out_ref.shape[2] // halves
    for half in range(halves):
        incoming = arrived.at[half, pl.ds(0, members - 1)]
        pltpu.make_async_copy(incoming, incoming, precv_sem.at[half]).wait()
        for row in range(rows):
            total = 0.0
            for source in range(members):
                total = total + arrived[half, source, row * piece : (row + 1) * piece, :].astype(
                    jnp.float32
                )
            gate, up = total[:, :columns], total[:, columns:]
            out_ref[row, :, half * columns : (half + 1) * columns] = (
                gate / (1.0 + jnp.exp(-gate)) * up
            ).astype(jnp.bfloat16)

    def finish(chunk, carry):
        others = states.at[chunk, :, :, pl.ds(0, span - piece), :]
        pltpu.make_async_copy(others, others, send_sem.at[chunk]).wait()
        for head in range(2):
            exchange(chunk, head).wait_send()

        @pl.when(has_up)
        def _():
            for copy in up_copies(chunk):
                copy.wait_send()

        @pl.when(has_down)
        def _():
            query_copy(chunk).wait_send()

        @pl.when(gives_down)
        def _():
            for copy in down_copies(chunk):
                copy.wait_send()

        return carry

    lax.fori_loop(0, chunks, finish, 0)
    for step in range(planes):

        @pl.when(jnp.logical_and(has_up, plane - step >= 0))
        def _():
            for half in range(halves):
                weight_copy(plane - step, half, weights.at[plane - step, half], 0, above).wait_send()

        @pl.when(jnp.logical_and(has_down, plane + step < planes))
        def _():
            for half in range(halves):
                weight_copy(plane + step, half, weights.at[plane + step, half], 1, below).wait_send()

    for half in range(halves):
        incoming = arrived.at[half, pl.ds(0, members - 1)]
        pltpu.make_async_copy(incoming, incoming, psend_sem.at[half]).wait()


def fused_body(queries, key_states, value_vectors, hypothesis_lengths, join_weight):
    rows, piece, width = (queries.shape[1], queries.shape[2], queries.shape[3])
    devices = lax.axis_size("seq")
    planes, members = devices // PACKED_ROWS, PACKED_ROWS
    head_width = width // ATTENTION_HEADS
    wide = 2 * head_width
    chunks = width // (members * wide)
    span = members * piece
    halves = 2
    weight_rows, _, columns = join_weight.shape
    part = columns // halves
    by_halves = jnp.transpose(join_weight.reshape(weight_rows, 2, halves, part), (2, 0, 1, 3))
    geometry = (planes, rows, members, piece, head_width, chunks, halves)

    def vmem(*shape):
        return pltpu.VMEM(shape, jnp.bfloat16)

    dma = pltpu.SemaphoreType.DMA
    context = (chunks, rows, span, wide)
    stats = (chunks, span, head_width)
    return pl.pallas_call(
        functools.partial(pair_kernel, geometry),
        out_shape=jax.ShapeDtypeStruct((rows, piece, columns), jnp.bfloat16),
        in_specs=[pl.BlockSpec(memory_space=pltpu.VMEM)] + [pl.BlockSpec(memory_space=pl.ANY)] * 4,
        out_specs=pl.BlockSpec(memory_space=pltpu.VMEM),
        scratch_shapes=[
            vmem(chunks, 3, rows, span, wide),
            vmem(*context),
            vmem(chunks, rows, 2 * span, wide + head_width),
            *[vmem(*context)] * 3,
            *[vmem(chunks, rows, span // 2, wide)] * 2,
            *[vmem(*stats)] * 3,
            *[vmem(chunks, span // 2, head_width)] * 2,
            vmem(planes, halves, weight_rows, 2 * part),
            vmem(chunks, members, rows * piece, 2 * wide),
            pltpu.VMEM((halves, members, rows * piece, 2 * part), jnp.float32),
            vmem(halves, members, rows * piece, 2 * part),
            vmem(halves, members, rows * piece, 2 * part),
            vmem(rows, span, 2 * span),
            vmem(rows, span, 2 * span),
            vmem(rows, span // 2, span),
            vmem(rows, span, span // 2),
            pltpu.VMEM((rows, span, span), jnp.float32),
            pltpu.VMEM((rows, span, span), jnp.float32),
            dma((chunks,)),
            dma((chunks,)),
            dma((chunks,)),
            dma((chunks,)),
            dma((chunks,)),
            dma((chunks, 2)),
            dma((chunks, 2)),
            dma((chunks, 2)),
            dma((chunks, 2)),
            dma((2, planes, halves)),
            dma((planes, halves)),
            dma,
            dma((chunks, 2)),
            dma((chunks, 2)),
            dma((halves,)),
            dma((halves,)),
        ],
        compiler_params=pltpu.CompilerParams(
            collective_id=0, has_side_effects=True, vmem_limit_bytes=60 * 1024 * 1024
        ),
    )(
        hypothesis_lengths,
        queries,
        key_states,
        value_vectors,
        by_halves.reshape(halves, weight_rows, 2 * part),
    )


def fits_kernel(mesh):
    planes = mesh.shape["seq"] // PACKED_ROWS
    return ATTENTION_HEADS // planes == 2 * PACKED_ROWS


def solution(mesh):
    return jax.shard_map(
        fused_body if fits_kernel(mesh) else body,
        mesh=mesh,
        in_specs=(
            P("dir", None, "seq", None),
            P("dir", None, "seq", None),
            P("dir", None, "seq", None),
            P(),
            P("seq", None, "dir"),
        ),
        out_specs=P(None, "seq", "dir"),
        check_vma=False,
    )
```
